256 devices in a mesh: bulk: 16 (over x_lo, y, core), wide: 16 (over x_hi, z).
Axes of the slice: x: 4 (x_hi: 2, x_lo: 2; x = x_hi * 2 + x_lo), y: 4, z: 8, core: 2. Of those that a mesh axis runs over, the one named last changes fastest.
Arguments:
- eps_corr: bfloat16 [2, 12288, 49152], P(None, 'bulk', 'wide'), may hold values from -0.00036621094 to 0.00036621094
- pair_rows: bfloat16 [2, 96, 12288], P(None, None, ('bulk', 'wide')), may hold values from -6 to 6
- pair_cols: bfloat16 [2, 96, 49152], P(None, None, ('wide', 'bulk')), may hold values from -6 to 6
- coulomb: float32 [49152], P(('wide', 'bulk')), may hold values from 0.3 to 3
- wing_row: bfloat16 [2, 49152], P(None, ('wide', 'bulk')), may hold values from -0.02734375 to 0.02734375
- wing_col: bfloat16 [2, 12288], P(None, ('bulk', 'wide')), may hold values from -0.0546875 to 0.0546875
- pair_head: float32 [2, 96], replicated, may hold values from -6 to 6
- head_value: float32 [2], replicated, may hold values from -4 to 4
- head_coulomb: float32 [1], replicated, may hold values from 0.5 to 2
- inner_bands: int32 [12], replicated, may hold values from 0 to 23
Outputs:
- self_energy: float32 [2, 8, 8], replicated
The draws below stay inside these ranges and needn't reach their ends.
All inputs are finite; a program needn't handle non-finite values.
Results may differ from the reference program's by a relative error of at most 0.002.
Values may be sent and summed in bfloat16 or wider, within the bound.
A program may use at most 64 MiB of HBM per device.

```python
import math
import jax
import jax.numpy as jnp
from jax import lax

NT = 8
NL = 12
PAIRS = 96
NWIN = 24
NVAL = 12
NG = 49152
ROWS = 12288
N_BULK = 16


def place_ends(result, own_key, low, high):
    index_at = [jax.random.randint(jax.random.fold_in(own_key, axis), (), 0, length) for axis, length in enumerate(result.shape)]
    main_axis = result.shape.index(max(result.shape))
    beside = index_at[:main_axis] + [(index_at[main_axis] + 1) % result.shape[main_axis]] + index_at[main_axis + 1:]
    return result.at[tuple(index_at)].set(low).at[tuple(beside)].set(high)


def spiked(values, stream_key, source, target, shards_of, factor):
    def block_of(position):
        return (jnp.arange(values.shape[position]) // (values.shape[position] // shards_of)).reshape((-1,) + (1,) * (values.ndim - 1 - position))

    near = jax.random.permutation(stream_key, shards_of)[block_of(target)]
    far = (block_of(target) + shards_of // 2) % shards_of
    return jnp.where((block_of(source) == near) | (block_of(source) == far), factor * values, values)


def block_scale(key, extent, pieces, least, high):
    def one(dim, parts):
        steps = jax.random.uniform(jax.random.fold_in(jax.random.fold_in(key, 6), dim), (parts,), jnp.float32, least / len(pieces), high / len(pieces))
        return jnp.repeat(jnp.exp(steps), extent[dim] // parts).reshape((-1,) + (1,) * (len(extent) - dim - 1))

    gain = one(*pieces[0])
    for cut in pieces[1:]:
        gain = gain * one(*cut)
    return gain


def normal_values(rng, shape, spread, most, split=(), kind=jnp.bfloat16):
    drawn = spread * jax.random.normal(rng, shape, jnp.float32)
    if split:
        drawn = drawn * block_scale(rng, shape, split, -0.22, 0.18)
    return jnp.clip(drawn, -most, most).astype(kind)


def noise_with(own_key, shape, width, most, shards, heavy, kind=jnp.bfloat16):
    array = width * jax.random.normal(own_key, shape, jnp.float32)
    if shards:
        array = array * block_scale(own_key, shape, shards, -0.22, 0.18)
    return jnp.clip(spiked(array, jax.random.fold_in(own_key, 3), *heavy), -most, most).astype(kind)


def setup_inputs(seed: int = 0) -> dict:
    splits = jax.random.split(jax.random.key(seed), 11)
    return {
        "eps_corr": noise_with(splits[0], (2, ROWS, NG), (ROWS * NG) ** -0.5, 0.00036621094, ((1, 16), (2, 16)), (2, 1, 16, 2.0)),
        "pair_rows": normal_values(splits[1], (2, PAIRS, ROWS), 1.0, 6.0, ((2, 256),)),
        "pair_cols": normal_values(splits[2], (2, PAIRS, NG), 1.0, 6.0, ((2, 256),)),
        "coulomb": jnp.clip(jnp.exp(math.log(3.0) - 2.3025851 * jax.random.uniform(splits[3], (NG,), jnp.float32) ** block_scale(splits[3], (NG,), ((0, 256),), -0.2, 0.2)), 0.3, 3.0),
        "wing_row": normal_values(splits[4], (2, NG), NG ** -0.5, 0.02734375, ((1, 256),)),
        "wing_col": normal_values(splits[5], (2, ROWS), ROWS ** -0.5, 0.0546875, ((1, 256),)),
        "pair_head": normal_values(splits[6], (2, PAIRS), 1.0, 6.0, (), jnp.float32),
        "head_value": normal_values(splits[7], (2,), 1.0, 4.0, (), jnp.float32),
        "head_coulomb": jnp.clip(jnp.exp(jax.random.uniform(splits[8], (1,), jnp.float32, math.log(0.5), math.log(2.0))), 0.5, 2.0),
        "inner_bands": place_ends(jax.random.randint(splits[9], (NL,), 0, NWIN), jax.random.fold_in(splits[9], 1), 0, NWIN - 1).astype(jnp.int32),
    }


def pair_sum(left_re, left_im, right_re, right_im, weights):
    layout = (NT, NL, -1)
    left_re = left_re.reshape(layout)
    left_im = left_im.reshape(layout)
    scaled_re = right_re.reshape(layout) * weights[None, :, None]
    scaled_im = right_im.reshape(layout) * weights[None, :, None]
    pattern = "nlx,mlx->nm"
    highest = lax.Precision.HIGHEST
    real_part = jnp.einsum(pattern, left_re, scaled_re, precision=highest) - jnp.einsum(pattern, left_im, scaled_im, precision=highest)
    imag_part = jnp.einsum(pattern, left_re, scaled_im, precision=highest) + jnp.einsum(pattern, left_im, scaled_re, precision=highest)
    return jnp.stack([real_part, imag_part])


def reference(eps_corr, pair_rows, pair_cols, coulomb, wing_row, wing_col, pair_head, head_value, head_coulomb, inner_bands):
    highest = lax.Precision.HIGHEST
    weights = jnp.where(inner_bands < NVAL, -0.5, 0.5).astype(jnp.float32)
    weighted = (coulomb[None, None, :] * pair_cols.astype(jnp.float32)).astype(jnp.bfloat16)
    weighted = lax.optimization_barrier(weighted)
    weighted_full = weighted.astype(jnp.float32)
    contract_last = (((1,), (1,)), ((), ()))
    block_rows = ROWS // N_BULK

    def block_term(running, number):
        offset = (number * block_rows).astype(jnp.int32)
        panel = lax.dynamic_slice_in_dim(eps_corr, offset, block_rows, 1).astype(jnp.float32)
        rows_here = lax.dynamic_slice_in_dim(pair_rows, offset, block_rows, 2).astype(jnp.float32)
        image_re = lax.dot_general(weighted_full[0], panel[0], contract_last, precision=highest) - lax.dot_general(weighted_full[1], panel[1], contract_last, precision=highest)
        image_im = lax.dot_general(weighted_full[0], panel[1], contract_last, precision=highest) + lax.dot_general(weighted_full[1], panel[0], contract_last, precision=highest)
        return running + pair_sum(rows_here[0], -rows_here[1], image_re, image_im, weights), None

    main_part, _ = lax.scan(block_term, jnp.zeros((2, NT, NT), jnp.float32), jnp.arange(N_BULK, dtype=jnp.int32))
    head_pairs = pair_head.astype(jnp.float32)
    wing_cols = wing_row.astype(jnp.float32)
    gain_re = jnp.dot(weighted_full[0], wing_cols[0], precision=highest) - jnp.dot(weighted_full[1], wing_cols[1], precision=highest)
    gain_im = jnp.dot(weighted_full[0], wing_cols[1], precision=highest) + jnp.dot(weighted_full[1], wing_cols[0], precision=highest)
    row_wing = pair_sum(head_pairs[0][:, None], -head_pairs[1][:, None], gain_re[:, None], gain_im[:, None], weights)
    rows_all = pair_rows.astype(jnp.float32)
    wing_rows = wing_col.astype(jnp.float32)
    tilt_re = jnp.dot(rows_all[0], wing_rows[0], precision=highest) + jnp.dot(rows_all[1], wing_rows[1], precision=highest)
    tilt_im = jnp.dot(rows_all[0], wing_rows[1], precision=highest) - jnp.dot(rows_all[1], wing_rows[0], precision=highest)
    coulomb_zero = head_coulomb[0]
    col_wing = pair_sum(tilt_re[:, None], tilt_im[:, None], coulomb_zero * head_pairs[0][:, None], coulomb_zero * head_pairs[1][:, None], weights)
    scaled_re = coulomb_zero * (head_value[0] * head_pairs[0] - head_value[1] * head_pairs[1])
    scaled_im = coulomb_zero * (head_value[0] * head_pairs[1] + head_value[1] * head_pairs[0])
    head_term = pair_sum(head_pairs[0], -head_pairs[1], scaled_re, scaled_im, weights)
    return main_part + row_wing + col_wing + head_term
```

```python
import jax
import jax.numpy as jnp
from jax import lax
from jax.experimental import pallas as pl
from jax.experimental.pallas import tpu as pltpu
from jax.sharding import PartitionSpec as P

NT = 8
NL = 12
NVAL = 12
PAIRS = 96
ROWS = 768
COLS = 3072
UNITS = 8
UNIT = 384
OWN = 192
OWN_ROWS = 48
WIDE = 16
BULK = 16
HIGHEST = lax.Precision.HIGHEST
MESH = pl.DeviceIdType.MESH
OFFSETS = ((0, 0), (1, 0), (0, 1), (0, 3), (1, 1), (1, 3), (0, 2), (1, 2))
CONTRACT_LAST = (((1,), (1,)), ((), ()))


def dot(a, b, **kw):
    return jnp.dot(a, b, preferred_element_type=jnp.float32, **kw)


def dot_t(a, b, **kw):
    return lax.dot_general(a, b, CONTRACT_LAST, preferred_element_type=jnp.float32, **kw)


def iota(shape, dim):
    return lax.broadcasted_iota(jnp.int32, shape, dim)


def kernel(
    eps_hbm,
    rows_hbm,
    cols_hbm,
    coulomb_hbm,
    wing_row_hbm,
    wing_col_hbm,
    head_hbm,
    head_value_ref,
    head_coulomb_ref,
    bands_ref,
    out_ref,
    eps,
    rows,
    cols,
    coulomb,
    wing_row,
    wing_col,
    head,
    parcels,
    row_blocks,
    image,
    spread_hi,
    spread_lo,
    base,
    part_a,
    part_b,
    eps_sem,
    in_sem,
    parcel_send,
    parcel_recv,
    pass_send,
    row_send,
    row_recv,
    a_send,
    a_recv,
    b_send,
    b_recv,
):
    bulk = lax.axis_index("bulk")
    wide = lax.axis_index("wide")
    core = lax.rem(bulk, 2)
    chip = lax.div(bulk, 2)
    x_lo = lax.div(chip, 4)
    y = lax.rem(chip, 4)

    def unit_at(dx, dy):
        return lax.rem(x_lo + dx, 2) * 4 + lax.rem(y + dy, 4)

    units = [unit_at(dx, dy) for dx, dy in OFFSETS]

    small = [
        pltpu.make_async_copy(src, dst, in_sem.at[i])
        for i, (src, dst) in enumerate(
            (
                (cols_hbm, cols),
                (coulomb_hbm, coulomb),
                (rows_hbm, rows),
                (head_hbm, head),
                (wing_row_hbm, wing_row),
                (wing_col_hbm, wing_col),
            )
        )
    ]
    for copy in small:
        copy.start()
    slabs = []
    for i, unit in enumerate(units):
        span = pl.ds(pl.multiple_of(unit * UNIT, 128), UNIT)
        copy = pltpu.make_async_copy(eps_hbm.at[:, :, span], eps.at[:, :, span], eps_sem.at[i])
        copy.start()
        slabs.append(copy)

    barrier = pltpu.get_barrier_semaphore()
    for k in range(1, BULK):
        pl.semaphore_signal(
            barrier, inc=1, device_id={"bulk": lax.rem(bulk + k, BULK), "wide": wide}, device_id_type=MESH
        )
    for k in range(1, WIDE):
        pl.semaphore_signal(
            barrier, inc=1, device_id={"bulk": bulk, "wide": lax.rem(wide + k, WIDE)}, device_id_type=MESH
        )

    small[0].wait()
    small[1].wait()
    weighted = coulomb[...][None] * cols[...].astype(jnp.float32)
    weighted_pairs = weighted.reshape(2 * PAIRS, OWN)
    first = core == 0
    main = jnp.where(first, weighted_pairs[:, 0:128], weighted_pairs[:, 64:192])
    near = jnp.where(first, weighted[0][:, 128:192], weighted[1][:, 0:64])
    far = jnp.where(first, weighted[1][:, 128:192], weighted[0][:, 0:64])
    mine = parcels.at[chip, core]
    mine[0:192, :] = main.astype(jnp.bfloat16)
    mine[192:288, :] = jnp.concatenate([near, far], axis=1).astype(jnp.bfloat16)
    small[2].wait()
    wide_rows = rows[...].astype(jnp.float32)
    gap = jnp.zeros((PAIRS, 16), jnp.float32)
    row_blocks[wide] = jnp.concatenate([wide_rows[0], gap, wide_rows[1], gap], axis=1).astype(jnp.bfloat16)

    pl.semaphore_wait(barrier, BULK + WIDE - 2)

    sends = []

    def send(src, dst, send_sem, recv_sem, to_bulk, to_wide):
        copy = pltpu.make_async_remote_copy(
            src_ref=src,
            dst_ref=dst,
            send_sem=send_sem,
            recv_sem=recv_sem,
            device_id={"bulk": to_bulk, "wide": to_wide},
            device_id_type=MESH,
        )
        copy.start()
        sends.append(copy)

    sibling = chip * 2 + 1 - core
    send(mine, mine, pass_send.at[0], parcel_recv.at[chip, core], sibling, wide)
    for i, unit in enumerate(units[1:]):
        send(mine, mine, parcel_send.at[i], parcel_recv.at[chip, core], unit * 2 + core, wide)
    for k in (1, 15, 8, 2, 14, 9, 7, 3, 13, 10, 6, 4, 12, 11, 5):
        place = row_blocks.at[wide]
        send(place, place, row_send.at[k], row_recv.at[wide], bulk, lax.rem(wide + k, WIDE))

    for copy in small[3:]:
        copy.wait()
    pair_re = head[0:1, :]
    pair_im = head[1:2, :]
    head_row = jnp.concatenate([pair_re, pair_im], axis=1)
    turned_row = jnp.concatenate([-pair_im, pair_re], axis=1)
    both = 2 * PAIRS
    diagonal = iota((both, both), 0) == iota((both, both), 1)
    head_col = jnp.sum(jnp.where(diagonal, head_row, 0.0), axis=1, keepdims=True)
    coulomb_zero = head_coulomb_ref[0]
    scaled_row = coulomb_zero * head_row
    scaled_turned = coulomb_zero * turned_row
    weighted_low = weighted_pairs.astype(jnp.bfloat16)
    weighted_turned = jnp.concatenate([-weighted_low[PAIRS:], weighted_low[:PAIRS]], axis=0)
    wing_cols = wing_row[...]
    gain = dot_t(wing_cols, weighted_low)[0:1] + dot_t(wing_cols, weighted_turned)[1:2]
    rows_own = wide_rows.reshape(both, OWN_ROWS)
    wing_rows = wing_col[...].astype(jnp.float32)
    tilt_re = jnp.sum(rows_own * wing_rows[0:1], axis=1, keepdims=True)
    tilt_im = jnp.sum(rows_own * wing_rows[1:2], axis=1, keepdims=True)
    leads = jnp.where(jnp.logical_and(bulk == 0, wide == 0), 1.0, 0.0)
    from_head = gain + leads * (head_value_ref[0] * scaled_row + head_value_ref[1] * scaled_turned)
    base[...] = head_col * from_head + tilt_re * scaled_row + tilt_im * scaled_turned

    left_l = lax.rem(iota((both, both), 0), NL)
    right_l = lax.rem(iota((both, both), 1), NL)
    lane_l = lax.rem(iota((1, both), 1), NL)
    weight_row = jnp.zeros((1, both), jnp.float32)
    for l in range(NL):
        weight_row = jnp.where(lane_l == l, jnp.where(bands_ref[l] < NVAL, -0.5, 0.5), weight_row)
    mask = jnp.where(left_l == right_l, weight_row, 0.0)

    blank = jnp.zeros((16, both), jnp.bfloat16)
    for k in range(2 * WIDE):
        spread_hi[64 * k + 48 : 64 * k + 64, :] = blank
        spread_lo[64 * k + 48 : 64 * k + 64, :] = blank

    low_lanes = iota((PAIRS, 128), 1) < 64

    def halves(unit):
        head_block = parcels[unit, 0, 0:192, :]
        tail_block = parcels[unit, 1, 0:192, :]
        half0 = parcels[unit, 0, 192:288, :].astype(jnp.float32)
        half1 = parcels[unit, 1, 192:288, :].astype(jnp.float32)
        mid_re = jnp.where(low_lanes, half0, half1)
        mid_im = pltpu.roll(jnp.where(low_lanes, half1, half0), 64, 1)
        middle = jnp.concatenate([mid_re, mid_im], axis=0).astype(jnp.bfloat16)
        straight = jnp.concatenate([head_block, middle, tail_block], axis=1)
        turned = jnp.concatenate([-straight[PAIRS:], straight[:PAIRS]], axis=0)
        return jnp.concatenate([straight, turned], axis=1)

    def arrived(unit, of_core):
        place = parcels.at[unit, of_core]
        pltpu.make_async_copy(place, place, parcel_recv.at[unit, of_core]).wait()

    for i, unit in enumerate(units):
        if i + 1 < UNITS:
            later = units[i + 1]
            arrived(later, core)
            place = parcels.at[later, core]
            send(place, place, pass_send.at[i + 1], parcel_recv.at[later, core], sibling, wide)
        arrived(unit, 1 - core)
        slabs[i].wait()
        span = pl.ds(pl.multiple_of(unit * UNIT, 128), UNIT)
        slab = jnp.concatenate([eps[0, :, span], eps[1, :, span]], axis=1)
        term = dot_t(slab, halves(unit))
        if i == 0:
            image[...] = term
        else:
            image[...] += term

    for k in range(WIDE):
        block = image[OWN_ROWS * k : OWN_ROWS * (k + 1), :]
        high = block.astype(jnp.bfloat16)
        low = (block - high.astype(jnp.float32)).astype(jnp.bfloat16)
        for at in (128 * k, 128 * k + 64):
            spread_hi[at : at + OWN_ROWS, :] = high
            spread_lo[at : at + OWN_ROWS, :] = low

    for k in range(1, WIDE):
        place = row_blocks.at[lax.rem(wide + k, WIDE)]
        pltpu.make_async_copy(place, place, row_recv.at[lax.rem(wide + k, WIDE)]).wait()
    zero = jnp.zeros((PAIRS, 128), jnp.bfloat16)
    blocks = [row_blocks[k] for k in range(WIDE)]
    left = jnp.concatenate(
        [
            jnp.concatenate([jnp.where(low_lanes, b, zero) for b in blocks], axis=1),
            jnp.concatenate([jnp.where(low_lanes, zero, b) for b in blocks], axis=1),
        ],
        axis=0,
    )
    pairs = mask * (base[...] + dot(left, spread_hi[...]) + dot(left, spread_lo[...]))

    band = lax.div(iota((2 * NT, both), 1), NL)
    gather_rows = jnp.where(band == iota((2 * NT, both), 0), 1.0, 0.0)
    by_rows = dot(gather_rows, pairs, precision=HIGHEST)
    lane = iota((both, 128), 1)
    of_pair = lax.div(iota((both, 128), 0), NL)
    same = jnp.where(lane == of_pair, 1.0, 0.0)
    crossed = jnp.where(lane == of_pair - NT, 1.0, 0.0) - jnp.where(lane == of_pair + NT, 1.0, 0.0)
    crossed = jnp.where(lane < 2 * NT, crossed, 0.0)
    share = dot(by_rows[0:NT], same, precision=HIGHEST) + dot(by_rows[NT:], crossed, precision=HIGHEST)

    part_a[bulk] = share
    for k in range(1, BULK):
        place = part_a.at[bulk]
        send(place, place, a_send.at[k], a_recv.at[bulk], lax.rem(bulk + k, BULK), wide)
    for k in range(1, BULK):
        place = part_a.at[lax.rem(bulk + k, BULK)]
        pltpu.make_async_copy(place, place, a_recv.at[lax.rem(bulk + k, BULK)]).wait()
    part_b[wide] = jnp.sum(part_a[...], axis=0)
    for k in range(1, WIDE):
        place = part_b.at[wide]
        send(place, place, b_send.at[k], b_recv.at[wide], bulk, lax.rem(wide + k, WIDE))
    for k in range(1, WIDE):
        place = part_b.at[lax.rem(wide + k, WIDE)]
        pltpu.make_async_copy(place, place, b_recv.at[lax.rem(wide + k, WIDE)]).wait()
    total = jnp.sum(part_b[...], axis=0)
    out_ref[0] = total[:, 0:NT]
    out_ref[1] = total[:, NT : 2 * NT]
    for copy in sends:
        copy.wait_send()


def local(eps_corr, pair_rows, pair_cols, coulomb, wing_row, wing_col, pair_head, head_value, head_coulomb, inner_bands):
    bf16, f32 = jnp.bfloat16, jnp.float32
    dma = pltpu.SemaphoreType.DMA
    return pl.pallas_call(
        kernel,
        out_shape=jax.ShapeDtypeStruct((2, NT, NT), f32),
        in_specs=[pl.BlockSpec(memory_space=pl.ANY)] * 7 + [pl.BlockSpec(memory_space=pltpu.SMEM)] * 3,
        out_specs=pl.BlockSpec(memory_space=pltpu.VMEM),
        scratch_shapes=[
            pltpu.VMEM((2, ROWS, COLS), bf16),
            pltpu.VMEM((2, PAIRS, OWN_ROWS), bf16),
            pltpu.VMEM((2, PAIRS, OWN), bf16),
            pltpu.VMEM((1, OWN), f32),
            pltpu.VMEM((2, OWN), bf16),
            pltpu.VMEM((2, OWN_ROWS), bf16),
            pltpu.VMEM((2, PAIRS), f32),
            pltpu.VMEM((UNITS, 2, 288, 128), bf16),
            pltpu.VMEM((WIDE, PAIRS, 128), bf16),
            pltpu.VMEM((ROWS, 2 * PAIRS), f32),
            pltpu.VMEM((WIDE * 128, 2 * PAIRS), bf16),
            pltpu.VMEM((WIDE * 128, 2 * PAIRS), bf16),
            pltpu.VMEM((2 * PAIRS, 2 * PAIRS), f32),
            pltpu.VMEM((BULK, NT, 128), f32),
            pltpu.VMEM((WIDE, NT, 128), f32),
            dma((UNITS,)),
            dma((6,)),
            dma((UNITS - 1,)),
            dma((UNITS, 2)),
            dma((UNITS,)),
            dma((WIDE,)),
            dma((WIDE,)),
            dma((BULK,)),
            dma((BULK,)),
            dma((WIDE,)),
            dma((WIDE,)),
        ],
        compiler_params=pltpu.CompilerParams(
            collective_id=0, has_side_effects=True, vmem_limit_bytes=40 * 1024 * 1024
        ),
    )(
        eps_corr,
        pair_rows,
        pair_cols,
        coulomb.reshape(1, OWN),
        wing_row,
        wing_col,
        pair_head,
        head_value,
        head_coulomb,
        inner_bands,
    )


def solution(mesh):
    placed = (
        P(None, "bulk", "wide"),
        P(None, None, ("bulk", "wide")),
        P(None, None, ("wide", "bulk")),
        P(("wide", "bulk")),
        P(None, ("wide", "bulk")),
        P(None, ("bulk", "wide")),
        P(),
        P(),
        P(),
        P(),
    )
    return jax.shard_map(local, mesh=mesh, in_specs=placed, out_specs=P(), check_vma=False)
```

```python
import jax
import jax.numpy as jnp
from jax import lax
from jax.experimental import pallas as pl
from jax.experimental.pallas import tpu as pltpu
from jax.sharding import PartitionSpec as P

NT = 8
NL = 12
NVAL = 12
PAIRS = 96
BOTH = 192
ROWS = 768
COLS = 3072
UNITS = 8
UNIT = 384
OWN = 192
OWN_ROWS = 48
N_Z = 8
WIDE = 16
BULK = 16
BLOCK = 80
CUT = 48
STEPS = (0, 1, -1, 2, -2, 3, -3, 4)
HIGHEST = lax.Precision.HIGHEST
MESH = pl.DeviceIdType.MESH
CONTRACT_LAST = (((1,), (1,)), ((), ()))


def dot(a, b, **kw):
    return jnp.dot(a, b, preferred_element_type=jnp.float32, **kw)


def dot_t(a, b, **kw):
    return lax.dot_general(a, b, CONTRACT_LAST, preferred_element_type=jnp.float32, **kw)


def iota(shape, dim):
    return lax.broadcasted_iota(jnp.int32, shape, dim)


def split(value):
    high = value.astype(jnp.bfloat16)
    return high, (value - high.astype(jnp.float32)).astype(jnp.bfloat16)


def kernel(
    eps_hbm,
    rows_hbm,
    cols_hbm,
    coulomb_hbm,
    wing_row_hbm,
    wing_col_hbm,
    head_hbm,
    head_value_hbm,
    head_coulomb_hbm,
    bands_hbm,
    out_ref,
    eps,
    rows,
    cols,
    coulomb,
    wing_row,
    wing_col,
    head,
    head_value_ref,
    head_coulomb_ref,
    bands_ref,
    parcels,
    row_blocks,
    rows_stack,
    rows_turned,
    order,
    fold,
    image,
    image_high,
    image_low,
    base,
    part_a,
    part_b,
    eps_sem,
    in_sem,
    parcel_send,
    parcel_recv,
    row_send,
    row_recv,
    a_send,
    a_recv,
    b_send,
    b_recv,
):
    bulk = lax.axis_index("bulk")
    wide = lax.axis_index("wide")
    core = lax.rem(bulk, 2)
    chip = lax.div(bulk, 2)
    x_lo = lax.div(chip, 4)
    y = lax.rem(chip, 4)
    x_hi = lax.div(wide, N_Z)
    z = lax.rem(wide, N_Z)

    def unit_at(dx, dy):
        return lax.rem(x_lo + dx, 2) * 4 + lax.rem(y + dy, 4)

    def z_at(dz):
        return lax.rem(z + dz + N_Z, N_Z)

    here, across = unit_at(0, 0), unit_at(1, 0)
    along = [unit_at(0, 1), unit_at(0, 3), unit_at(0, 2)]
    aslant = [unit_at(1, 1), unit_at(1, 3), unit_at(1, 2)]
    units = [here, across] + along + aslant

    small = [
        pltpu.make_async_copy(src, dst, in_sem.at[i])
        for i, (src, dst) in enumerate(
            (
                (rows_hbm, rows),
                (cols_hbm, cols),
                (coulomb_hbm, coulomb),
                (head_hbm, head),
                (wing_row_hbm, wing_row),
                (wing_col_hbm, wing_col),
                (head_value_hbm, head_value_ref),
                (head_coulomb_hbm, head_coulomb_ref),
                (bands_hbm, bands_ref),
            )
        )
    ]
    for copy in small:
        copy.start()

    sibling = chip * 2 + 1 - core
    across_x = lax.rem(x_hi + 1, 2) * N_Z + z

    def along_z(dz):
        return x_hi * N_Z + z_at(dz)

    barrier = pltpu.get_barrier_semaphore()
    greeted = [(bulk, across_x), (sibling, wide)]
    greeted += [(unit * 2 + core, wide) for unit in [across] + along]
    greeted += [(bulk, along_z(dz)) for dz in (1, -1, 2, -2)]
    for to_bulk, to_wide in greeted:
        pl.semaphore_signal(barrier, inc=1, device_id={"bulk": to_bulk, "wide": to_wide}, device_id_type=MESH)

    slabs = []
    for i, unit in enumerate(units):
        span = pl.ds(pl.multiple_of(unit * UNIT, 128), UNIT)
        copy = pltpu.make_async_copy(eps_hbm.at[:, :, span], eps.at[:, :, span], eps_sem.at[i])
        copy.start()
        slabs.append(copy)

    small[0].wait()
    rows_f32 = rows[...].astype(jnp.float32)
    rows_own = jnp.concatenate([rows_f32[0], rows_f32[1]], axis=1)
    mine_rows = row_blocks.at[wide]
    mine_rows[0:48] = rows_own[:, :128].astype(jnp.bfloat16)
    packed = jnp.concatenate([rows_own[0:24, 128:], rows_own[24:48, 128:]], axis=1)
    mine_rows[48:80] = jnp.concatenate([packed, jnp.zeros((8, 128), jnp.float32)], axis=0).astype(jnp.bfloat16)
    small[1].wait()
    small[2].wait()
    weighted = coulomb[...][None] * cols[...].astype(jnp.float32)
    weighted_pairs = weighted.reshape(BOTH, OWN)
    first = core == 0
    main = jnp.where(first, weighted_pairs[:, 0:128], weighted_pairs[:, 64:192])
    near = jnp.where(first, weighted[0][:, 128:192], weighted[1][:, 0:64])
    far = jnp.where(first, weighted[1][:, 128:192], weighted[0][:, 0:64])
    mine = parcels.at[bulk]
    mine[0:192, :] = main.astype(jnp.bfloat16)
    mine[192:288, :] = jnp.concatenate([near, far], axis=1).astype(jnp.bfloat16)

    pl.semaphore_wait(barrier, len(greeted))

    def send(place, send_sem, recv_sem, to_bulk, to_wide):
        pltpu.make_async_remote_copy(
            src_ref=place,
            dst_ref=place,
            send_sem=send_sem,
            recv_sem=recv_sem,
            device_id={"bulk": to_bulk, "wide": to_wide},
            device_id_type=MESH,
        ).start()

    def landed(place, sem):
        pltpu.make_async_copy(place, place, sem).wait()

    def send_parcel(of_bulk, to_bulk):
        send(parcels.at[of_bulk], parcel_send, parcel_recv.at[of_bulk], to_bulk, wide)

    def arrived(unit, of_core):
        at = unit * 2 + of_core
        landed(parcels.at[at], parcel_recv.at[at])

    def hand_on(unit):
        send_parcel(unit * 2 + core, sibling)

    def relay(unit, to_chip):
        send_parcel(unit * 2 + core, to_chip * 2 + core)

    def send_rows(of_wide, to_wide):
        send(row_blocks.at[of_wide], row_send, row_recv.at[of_wide, 0], bulk, to_wide)

    def rows_landed(of_wide):
        landed(row_blocks.at[of_wide], row_recv.at[of_wide, 0])

    send_rows(wide, across_x)
    relay(here, across)
    for dz in (2, -2, 1, -1):
        send_rows(wide, along_z(dz))
    for unit in along:
        relay(here, unit)
    hand_on(here)

    low_lanes = iota((PAIRS, 128), 1) < 64

    rows_landed(across_x)
    for dz in (2, -2, 1, -1):
        send_rows(across_x, along_z(dz))

    @pl.when(core == 0)
    def _():
        arrived(across, core)
        for unit in (along[2], along[0], along[1]):
            relay(across, unit)

    @pl.when(core == 1)
    def _():
        for unit in along[:2]:
            arrived(unit, core)
            relay(unit, across)
        arrived(across, core)

    hand_on(across)

    for copy in small[3:]:
        copy.wait()
    pair_re = head[0:1, :]
    pair_im = head[1:2, :]
    head_row = jnp.concatenate([pair_re, pair_im], axis=1)
    turned_row = jnp.concatenate([-pair_im, pair_re], axis=1)
    square = (BOTH, BOTH)
    row_at, lane_at = iota(square, 0), iota(square, 1)
    head_col = jnp.sum(jnp.where(row_at == lane_at, head_row, 0.0), axis=1, keepdims=True)
    coulomb_zero = head_coulomb_ref[0]
    scaled_row = coulomb_zero * head_row
    scaled_turned = coulomb_zero * turned_row
    weighted_low = (coulomb[...][None] * cols[...].astype(jnp.float32)).astype(jnp.bfloat16).reshape(BOTH, OWN)
    weighted_turned = jnp.concatenate([-weighted_low[PAIRS:], weighted_low[:PAIRS]], axis=0)
    wing_cols = wing_row[...]
    gain = dot_t(wing_cols, weighted_low)[0:1] + dot_t(wing_cols, weighted_turned)[1:2]
    rows_here = jnp.swapaxes(rows[...].astype(jnp.float32), 1, 2).reshape(BOTH, OWN_ROWS)
    wing_rows = wing_col[...].astype(jnp.float32)
    tilt_re = jnp.sum(rows_here * wing_rows[0:1], axis=1, keepdims=True)
    tilt_im = jnp.sum(rows_here * wing_rows[1:2], axis=1, keepdims=True)
    leads = jnp.where(jnp.logical_and(bulk == 0, wide == 0), 1.0, 0.0)
    from_head = gain + leads * (head_value_ref[0] * scaled_row + head_value_ref[1] * scaled_turned)
    outer = head_col * from_head + tilt_re * scaled_row + tilt_im * scaled_turned
    lane_l = lax.rem(iota((1, BOTH), 1), NL)
    weight_row = jnp.zeros((1, BOTH), jnp.float32)
    for l in range(NL):
        weight_row = jnp.where(lane_l == l, jnp.where(bands_ref[l] < NVAL, -0.5, 0.5), weight_row)
    outer = jnp.where(lax.rem(row_at, NL) == lax.rem(lane_at, NL), weight_row * outer, 0.0)

    pick = (BOTH, 128)
    from_q, to_lane = iota(pick, 0), iota(pick, 1)
    same_band = lax.div(lax.rem(from_q, PAIRS), NL) == lax.rem(to_lane, NT)
    part_q, part_lane = lax.div(from_q, PAIRS), lax.div(to_lane, 64)
    straight = jnp.where(jnp.logical_and(same_band, part_q == part_lane), 1.0, 0.0)
    sign = jnp.where(part_lane == 0, 1.0, -1.0)
    crossed = jnp.where(jnp.logical_and(same_band, part_q != part_lane), sign, 0.0)
    fold[0] = straight.astype(jnp.bfloat16)
    fold[1] = crossed.astype(jnp.bfloat16)
    band_lanes = lax.rem(lax.div(iota((NT, 128), 1), NT), NT) == iota((NT, 128), 0)
    band = lax.div(iota((2 * NT, BOTH), 1), NL)
    gather_rows = jnp.where(band == iota((2 * NT, BOTH), 0), 1.0, 0.0)
    by_rows = dot(gather_rows, outer, precision=HIGHEST)
    base[...] = dot(by_rows[0:NT], straight, precision=HIGHEST) + dot(by_rows[NT:], crossed, precision=HIGHEST)
    same_l = lax.rem(lane_at, NL) == lax.div(lax.rem(row_at, PAIRS), NT)
    same_n = lax.div(lax.rem(lane_at, PAIRS), NL) == lax.rem(row_at, NT)
    same_part = lax.div(lane_at, PAIRS) == lax.div(row_at, PAIRS)
    chosen = jnp.logical_and(jnp.logical_and(same_l, same_n), same_part)
    order[...] = jnp.where(chosen, weight_row, 0.0).astype(jnp.bfloat16)

    def work(i):
        unit = units[i]
        arrived(unit, 1 - core)
        slabs[i].wait()
        head_block = parcels[unit * 2, 0:192, :]
        tail_block = parcels[unit * 2 + 1, 0:192, :]
        half0 = parcels[unit * 2, 192:288, :]
        half1 = parcels[unit * 2 + 1, 192:288, :]
        mid_re = jnp.where(low_lanes, half0, half1)
        mid_im = jnp.where(low_lanes, half1, half0)
        mid_im = jnp.concatenate([mid_im[:, 64:], mid_im[:, :64]], axis=1)
        middle = jnp.concatenate([mid_re, mid_im], axis=0)
        plain = jnp.concatenate([head_block, middle, tail_block], axis=1)
        turned = jnp.concatenate([-plain[PAIRS:], plain[:PAIRS]], axis=0)
        span = pl.ds(pl.multiple_of(unit * UNIT, 128), UNIT)
        slab = jnp.concatenate([eps[0, :, span], eps[1, :, span]], axis=1)
        term = dot_t(slab, jnp.concatenate([plain, turned], axis=1))
        if i == 0:
            image[...] = term
        else:
            image[...] += term

    work(0)

    for at_x in (x_hi, lax.rem(x_hi + 1, 2)):
        for i, dz in enumerate((1, -1)):
            source = at_x * N_Z + z_at(-2 * dz)
            rows_landed(source)
            piece = row_blocks.at[source, pl.ds(0, CUT) if dz == 1 else pl.ds(CUT, BLOCK - CUT)]
            send(piece, row_send, row_recv.at[source, i], bulk, along_z(2 * dz))
            send_rows(source, along_z(dz))

    @pl.when(core == 0)
    def _():
        for unit in along:
            arrived(unit, core)

    @pl.when(core == 1)
    def _():
        arrived(along[2], core)
        relay(along[2], across)

    for unit in along:
        hand_on(unit)

    for i in (1, 2, 3, 4):
        work(i)

    for unit in aslant:
        arrived(unit, core)
        hand_on(unit)

    def turn_rows(batch):
        for j in range(4 * batch, 4 * batch + 4):
            for half in range(2):
                source = half * N_Z + z_at(STEPS[j])
                at = 96 * j + 48 * half
                packed = row_blocks[source, 48:72, :].astype(jnp.float32)
                rest = jnp.concatenate([packed, pltpu.roll(packed, 64, 1)], axis=0)
                rows_stack[at : at + 48, 0:128] = row_blocks[source, 0:48, :]
                rows_stack[at : at + 48, 128:256] = rest.astype(jnp.bfloat16)
        span = slice(384 * batch, 384 * batch + 384)
        rows_turned[:, span] = dot_t(order[...], rows_stack[span, 0:BOTH]).astype(jnp.bfloat16)

    for dz in (1, -1):
        for half in range(2):
            rows_landed(half * N_Z + z_at(dz))
    turn_rows(0)

    for i in (5, 6, 7):
        work(i)

    def split_image(batch):
        for j in range(4 * batch, 4 * batch + 4):
            for half in range(2):
                source = half * N_Z + z_at(STEPS[j])
                at = 96 * j + 48 * half
                block = image[pl.ds(pl.multiple_of(source * OWN_ROWS, 16), OWN_ROWS), :]
                image_high[at : at + 48, :], image_low[at : at + 48, :] = split(block)

    def multiply(batch):
        span = slice(384 * batch, 384 * batch + 384)
        left = rows_turned[:, span]
        return dot(left, image_high[span, :]) + dot(left, image_low[span, :])

    split_image(0)
    split_image(1)
    for half in range(2):
        for dz in (3, -3):
            rows_landed(half * N_Z + z_at(dz))
        source = half * N_Z + z_at(4)
        landed(row_blocks.at[source, pl.ds(0, CUT)], row_recv.at[source, 0])
        landed(row_blocks.at[source, pl.ds(CUT, BLOCK - CUT)], row_recv.at[source, 1])
    turn_rows(1)
    pairs = multiply(0) + multiply(1)
    total = base[...]
    for half in range(2):
        kept = jnp.zeros((NT, BOTH), jnp.float32)
        for l in range(NL):
            at = PAIRS * half + NT * l
            kept = jnp.where(lane_l == l, pairs[at : at + NT, :], kept)
        high, low = split(kept)
        total = total + dot(high, fold[half]) + dot(low, fold[half])
    share = jnp.sum(jnp.where(band_lanes, total, 0.0), axis=0, keepdims=True)

    part_a[bulk] = share
    for k in (7, 15, 5, 13, 6, 14, 1, 3, 9, 11, 2, 4, 8, 10, 12):
        send(part_a.at[bulk], a_send, a_recv, lax.rem(bulk + k, BULK), wide)
    landed(parcels.at[pl.ds(0, 15)], parcel_send)
    landed(row_blocks.at[pl.ds(0, 15)], row_send)
    landed(part_a.at[pl.ds(0, BULK - 1)], a_recv)
    part_b[wide] = jnp.sum(part_a[...], axis=0)
    for k in (12, 4, 11, 13, 3, 5, 10, 14, 2, 6, 9, 15, 1, 7, 8):
        send(part_b.at[wide], b_send, b_recv, bulk, lax.rem(wide + k, WIDE))
    landed(part_a.at[pl.ds(0, BULK - 1)], a_send)
    landed(part_b.at[pl.ds(0, WIDE - 1)], b_recv)
    result = jnp.where(band_lanes, jnp.sum(part_b[...], axis=0), 0.0)
    lanes = iota((NT, 128), 1)
    for part in range(2):
        value = jnp.where(lax.div(lanes, 64) == part, result, 0.0)
        for shift in (8, 16, 32, 64):
            value = value + pltpu.roll(value, shift, 1)
        out_ref[part] = value[:, 0:NT]
    landed(part_b.at[pl.ds(0, WIDE - 1)], b_send)


def local(eps_corr, pair_rows, pair_cols, coulomb, wing_row, wing_col, pair_head, head_value, head_coulomb, inner_bands):
    bf16, f32 = jnp.bfloat16, jnp.float32
    dma = pltpu.SemaphoreType.DMA
    return pl.pallas_call(
        kernel,
        out_shape=jax.ShapeDtypeStruct((2, NT, NT), f32),
        in_specs=[pl.BlockSpec(memory_space=pltpu.HBM)] * 10,
        out_specs=pl.BlockSpec(memory_space=pltpu.VMEM),
        scratch_shapes=[
            pltpu.VMEM((2, ROWS, COLS), bf16),
            pltpu.VMEM((2, OWN_ROWS, PAIRS), bf16),
            pltpu.VMEM((2, PAIRS, OWN), bf16),
            pltpu.VMEM((1, OWN), f32),
            pltpu.VMEM((2, OWN), bf16),
            pltpu.VMEM((2, OWN_ROWS), bf16),
            pltpu.VMEM((2, PAIRS), f32),
            pltpu.SMEM((2,), f32),
            pltpu.SMEM((1,), f32),
            pltpu.SMEM((NL,), jnp.int32),
            pltpu.VMEM((BULK, 288, 128), bf16),
            pltpu.VMEM((WIDE, BLOCK, 128), bf16),
            pltpu.VMEM((ROWS, 256), bf16),
            pltpu.VMEM((BOTH, ROWS), bf16),
            pltpu.VMEM((BOTH, BOTH), bf16),
            pltpu.VMEM((2, BOTH, 128), bf16),
            pltpu.VMEM((ROWS, BOTH), f32),
            pltpu.VMEM((ROWS, BOTH), bf16),
            pltpu.VMEM((ROWS, BOTH), bf16),
            pltpu.VMEM((NT, 128), f32),
            pltpu.VMEM((16, 1, 128), f32),
            pltpu.VMEM((16, 1, 128), f32),
            dma((UNITS,)),
            dma((9,)),
            dma,
            dma((BULK,)),
            dma,
            dma((WIDE, 2)),
            dma,
            dma,
            dma,
            dma,
        ],
        compiler_params=pltpu.CompilerParams(
            collective_id=0, has_side_effects=True, vmem_limit_bytes=63 * 1024 * 1024
        ),
    )(
        eps_corr,
        jnp.swapaxes(pair_rows, 1, 2),
        pair_cols,
        coulomb.reshape(1, OWN),
        wing_row,
        wing_col,
        pair_head,
        head_value,
        head_coulomb,
        inner_bands,
    )


def solution(mesh):
    placed = (
        P(None, "bulk", "wide"),
        P(None, None, ("bulk", "wide")),
        P(None, None, ("wide", "bulk")),
        P(("wide", "bulk")),
        P(None, ("wide", "bulk")),
        P(None, ("bulk", "wide")),
        P(),
        P(),
        P(),
        P(),
    )
    return jax.shard_map(local, mesh=mesh, in_specs=placed, out_specs=P(), check_vma=False)
```

```python
import jax
import jax.numpy as jnp
from jax import lax
from jax.experimental import pallas as pl
from jax.experimental.pallas import tpu as pltpu
from jax.sharding import PartitionSpec as P

NT = 8
NL = 12
NVAL = 12
PAIRS = 96
BOTH = 192
ROWS = 768
COLS = 3072
UNITS = 8
UNIT = 384
OWN = 192
OWN_ROWS = 48
N_Z = 8
WIDE = 16
BULK = 16
BLOCK = 80
CUT = 48
STEPS = (0, 1, -1, 2, -2, 3, -3, 4)
HIGHEST = lax.Precision.HIGHEST
MESH = pl.DeviceIdType.MESH
CONTRACT_LAST = (((1,), (1,)), ((), ()))


def dot(a, b, **kw):
    return jnp.dot(a, b, preferred_element_type=jnp.float32, **kw)


def dot_t(a, b, **kw):
    return lax.dot_general(a, b, CONTRACT_LAST, preferred_element_type=jnp.float32, **kw)


def iota(shape, dim):
    return lax.broadcasted_iota(jnp.int32, shape, dim)


def split(value):
    high = value.astype(jnp.bfloat16)
    return high, (value - high.astype(jnp.float32)).astype(jnp.bfloat16)


def kernel(
    eps_hbm,
    rows_hbm,
    cols_hbm,
    coulomb_hbm,
    wing_row_hbm,
    wing_col_hbm,
    head_hbm,
    head_value_hbm,
    head_coulomb_hbm,
    bands_hbm,
    out_ref,
    eps,
    rows,
    cols,
    coulomb,
    wing_row,
    wing_col,
    head,
    head_value_ref,
    head_coulomb_ref,
    bands_ref,
    parcels,
    own_weighted,
    row_blocks,
    rows_stack,
    rows_turned,
    order,
    fold,
    image,
    image_high,
    image_low,
    base,
    part_a,
    part_b,
    eps_sem,
    in_sem,
    parcel_send,
    parcel_recv,
    row_send,
    row_recv,
    a_send,
    a_recv,
    b_send,
    b_recv,
):
    bulk = lax.axis_index("bulk")
    wide = lax.axis_index("wide")
    core = lax.rem(bulk, 2)
    chip = lax.div(bulk, 2)
    x_lo = lax.div(chip, 4)
    y = lax.rem(chip, 4)
    x_hi = lax.div(wide, N_Z)
    z = lax.rem(wide, N_Z)

    def unit_at(dx, dy):
        return lax.rem(x_lo + dx, 2) * 4 + lax.rem(y + dy, 4)

    def unit_of(i):
        return unit_at(lax.div(i, 4), lax.rem(i, 4))

    def z_at(dz):
        return lax.rem(z + dz + N_Z, N_Z)

    here, across = unit_at(0, 0), unit_at(1, 0)

    def repeat(first, last, step):
        def body(i, carry):
            step(i)
            return carry

        lax.fori_loop(first, last, body, 0)

    small = [
        pltpu.make_async_copy(src, dst, in_sem.at[i])
        for i, (src, dst) in enumerate(
            (
                (rows_hbm, rows),
                (cols_hbm, cols),
                (coulomb_hbm, coulomb),
                (head_hbm, head),
                (wing_row_hbm, wing_row),
                (wing_col_hbm, wing_col),
                (head_value_hbm, head_value_ref),
                (head_coulomb_hbm, head_coulomb_ref),
                (bands_hbm, bands_ref),
            )
        )
    ]
    for copy in small:
        copy.start()

    sibling = chip * 2 + 1 - core
    across_x = lax.rem(x_hi + 1, 2) * N_Z + z

    def along_z(dz):
        return x_hi * N_Z + z_at(dz)

    barrier = pltpu.get_barrier_semaphore()

    def greet(to_bulk, to_wide):
        pl.semaphore_signal(barrier, inc=1, device_id={"bulk": to_bulk, "wide": to_wide}, device_id_type=MESH)

    greet(bulk, across_x)
    greet(sibling, wide)
    greet(across * 2 + core, wide)
    for dy in (1, 3, 2):
        greet(unit_at(0, dy) * 2 + core, wide)
    for dz in (1, -1, 2, -2):
        greet(bulk, along_z(dz))

    def slab(i):
        span = pl.ds(pl.multiple_of(unit_of(i) * UNIT, 128), UNIT)
        return pltpu.make_async_copy(eps_hbm.at[:, :, span], eps.at[i], eps_sem.at[i])

    repeat(0, UNITS, lambda i: slab(i).start())

    pl.semaphore_wait(barrier, 10)

    def send(place, send_sem, recv_sem, to_bulk, to_wide):
        pltpu.make_async_remote_copy(
            src_ref=place,
            dst_ref=place,
            send_sem=send_sem,
            recv_sem=recv_sem,
            device_id={"bulk": to_bulk, "wide": to_wide},
            device_id_type=MESH,
        ).start()

    def landed(place, sem):
        pltpu.make_async_copy(place, place, sem).wait()

    def send_parcel(of_bulk, to_bulk):
        send(parcels.at[of_bulk], parcel_send, parcel_recv.at[of_bulk], to_bulk, wide)

    def arrived(unit, of_core):
        at = unit * 2 + of_core
        landed(parcels.at[at], parcel_recv.at[at])

    def hand_on(unit):
        send_parcel(unit * 2 + core, sibling)

    def relay(unit, to_chip):
        send_parcel(unit * 2 + core, to_chip * 2 + core)

    def send_rows(of_wide, to_wide):
        send(row_blocks.at[of_wide], row_send, row_recv.at[of_wide, 0], bulk, to_wide)

    def rows_landed(of_wide):
        landed(row_blocks.at[of_wide], row_recv.at[of_wide, 0])

    small[0].wait()
    rows_f32 = rows[...].astype(jnp.float32)
    rows_own = jnp.concatenate([rows_f32[0], rows_f32[1]], axis=1)
    mine_rows = row_blocks.at[wide]
    rows_low = rows_own.astype(jnp.bfloat16)
    mine_rows[0:48] = rows_low[:, :128]
    packed = jnp.concatenate([rows_own[0:24, 128:], rows_own[24:48, 128:]], axis=1)
    mine_rows[48:80] = jnp.concatenate([packed, jnp.zeros((8, 128), jnp.float32)], axis=0).astype(jnp.bfloat16)
    send_rows(wide, across_x)
    small[1].wait()
    small[2].wait()
    weighted = coulomb[...][None] * cols[...].astype(jnp.float32)
    weighted_pairs = weighted.reshape(BOTH, OWN)
    first = core == 0
    main = jnp.where(first, weighted_pairs[:, 0:128], weighted_pairs[:, 64:192])
    near = jnp.where(first, weighted[0][:, 128:192], weighted[1][:, 0:64])
    far = jnp.where(first, weighted[1][:, 128:192], weighted[0][:, 0:64])
    mine = parcels.at[bulk]
    mine[0:192, :] = main.astype(jnp.bfloat16)
    own_weighted[...] = weighted_pairs.astype(jnp.bfloat16)
    mine[192:288, :] = jnp.concatenate([near, far], axis=1).astype(jnp.bfloat16)


    relay(here, across)

    def send_along(of_wide):
        def step(i):
            send_rows(of_wide, along_z(jnp.where(i < 2, i - 2, i - 1)))

        repeat(0, 4, step)

    send_along(wide)
    repeat(1, 4, lambda dy: relay(here, unit_at(0, dy)))
    hand_on(here)

    low_lanes = iota((PAIRS, 128), 1) < 64

    for copy in small[3:]:
        copy.wait()
    pair_re = head[0:1, :]
    pair_im = head[1:2, :]
    head_row = jnp.concatenate([pair_re, pair_im], axis=1)
    turned_row = jnp.concatenate([-pair_im, pair_re], axis=1)
    coulomb_zero = head_coulomb_ref[0]
    scaled_row = coulomb_zero * head_row
    scaled_turned = coulomb_zero * turned_row
    weighted_low = own_weighted[...]
    weighted_turned = jnp.concatenate([-weighted_low[PAIRS:], weighted_low[:PAIRS]], axis=0)
    wing_cols = wing_row[...]
    gain = dot_t(wing_cols, weighted_low)[0:1] + dot_t(wing_cols, weighted_turned)[1:2]
    tilt = dot(wing_col[...], rows_low)
    leads = jnp.where(jnp.logical_and(bulk == 0, wide == 0), 1.0, 0.0)
    from_head = gain + leads * (head_value_ref[0] * scaled_row + head_value_ref[1] * scaled_turned)
    lane = iota((1, BOTH), 1)
    lane_l = lax.rem(lane, NL)
    lane_band = lax.div(lane, NL)
    weight_row = jnp.zeros((1, BOTH), jnp.float32)
    for l in range(NL):
        weight_row = jnp.where(lane_l == l, jnp.where(bands_ref[l] < NVAL, -0.5, 0.5), weight_row)
    row_at = iota((BOTH, 1), 0)
    same_l = jnp.where(lax.rem(row_at, NL) == lane_l, weight_row, 0.0).astype(jnp.bfloat16)
    in_band = iota((2 * NT, BOTH), 0) == lane_band

    def gathered(row):
        spread = jnp.where(in_band, row, 0.0)
        high = spread.astype(jnp.bfloat16)
        middle, low = split(spread - high.astype(jnp.float32))
        return dot(high, same_l) + dot(middle, same_l) + dot(low, same_l)

    base[...] = (
        gathered(head_row) * from_head + gathered(tilt[0:1]) * scaled_row + gathered(tilt[1:2]) * scaled_turned
    )

    to_lane = iota((1, 128), 1)
    low_part = to_lane < 64
    key = jnp.where(low_part, 0, NT) + lax.rem(to_lane, NT)
    row_band = lax.div(row_at, NL)
    fold[0] = jnp.where(row_band == key, 1.0, 0.0).astype(jnp.bfloat16)
    sign = jnp.where(low_part, 1.0, -1.0)
    fold[1] = jnp.where(row_band == jnp.where(low_part, key + NT, key - NT), sign, 0.0).astype(jnp.bfloat16)
    band_lanes = lax.rem(lax.div(to_lane, NT), NT) == iota((NT, 128), 0)
    lane_half = lax.div(lane, PAIRS)
    place = lane_half * PAIRS + lane_l * NT + lane_band - lane_half * NT
    order[...] = jnp.where(iota((BOTH, BOTH), 0) == place, weight_row, 0.0).astype(jnp.bfloat16)
    image[...] = jnp.zeros((ROWS, BOTH), jnp.float32)

    rows_landed(across_x)
    send_along(across_x)

    @pl.when(core == 0)
    def _():
        arrived(across, core)
        repeat(1, 4, lambda dy: relay(across, unit_at(0, dy)))

    @pl.when(core == 1)
    def _():
        for dy in (1, 3):
            arrived(unit_at(0, dy), core)
            relay(unit_at(0, dy), across)
        arrived(across, core)

    hand_on(across)

    def work(i):
        unit = unit_of(i)
        arrived(unit, 1 - core)
        slab(i).wait()
        head_block = parcels[unit * 2, 0:192, :]
        tail_block = parcels[unit * 2 + 1, 0:192, :]
        half0 = parcels[unit * 2, 192:288, :]
        half1 = parcels[unit * 2 + 1, 192:288, :]
        mid_re = jnp.where(low_lanes, half0, half1)
        mid_im = jnp.where(low_lanes, half1, half0)
        mid_im = jnp.concatenate([mid_im[:, 64:], mid_im[:, :64]], axis=1)
        middle = jnp.concatenate([mid_re, mid_im], axis=0)
        plain = jnp.concatenate([head_block, middle, tail_block], axis=1)
        turned = jnp.concatenate([-plain[PAIRS:], plain[:PAIRS]], axis=0)
        left = jnp.concatenate([eps[i, 0], eps[i, 1]], axis=1)
        image[...] += dot_t(left, jnp.concatenate([plain, turned], axis=1))

    def relay_rows(at_x):
        for i, dz in enumerate((1, -1)):
            source = at_x * N_Z + z_at(-2 * dz)
            rows_landed(source)
            piece = row_blocks.at[source, pl.ds(0, CUT) if dz == 1 else pl.ds(CUT, BLOCK - CUT)]
            send(piece, row_send, row_recv.at[source, i], bulk, along_z(2 * dz))
            send_rows(source, along_z(dz))

    def second_stage():
        @pl.when(core == 0)
        def _():
            for dy in (1, 2, 3):
                arrived(unit_at(0, dy), core)

        @pl.when(core == 1)
        def _():
            arrived(unit_at(0, 2), core)
            relay(unit_at(0, 2), across)

        relay_rows(x_hi)
        repeat(1, 4, lambda dy: hand_on(unit_at(0, dy)))
        relay_rows(lax.rem(x_hi + 1, 2))

    def third_stage():
        def step(dy):
            arrived(unit_at(1, dy), core)
            hand_on(unit_at(1, dy))

        repeat(1, 4, step)

    def turn_rows(batch):
        for j in range(4 * batch, 4 * batch + 4):
            for half in range(2):
                source = half * N_Z + z_at(STEPS[j])
                at = 96 * j + 48 * half
                packed = row_blocks[source, 48:72, :].astype(jnp.float32)
                rest = jnp.concatenate([packed, pltpu.roll(packed, 64, 1)], axis=0)
                rows_stack[at : at + 48, 0:128] = row_blocks[source, 0:48, :]
                rows_stack[at : at + 48, 128:256] = rest.astype(jnp.bfloat16)
        span = slice(384 * batch, 384 * batch + 384)
        rows_turned[:, span] = dot_t(order[...], rows_stack[span, 0:BOTH]).astype(jnp.bfloat16)

    def units_step(i):
        @pl.when(i == 1)
        def _():
            second_stage()

        @pl.when(i == 5)
        def _():
            third_stage()

        work(i)

    repeat(0, UNITS, units_step)

    for dz in (1, -1):
        for half in range(2):
            rows_landed(half * N_Z + z_at(dz))
    turn_rows(0)

    def split_image(batch):
        for j in range(4 * batch, 4 * batch + 4):
            for half in range(2):
                source = half * N_Z + z_at(STEPS[j])
                at = 96 * j + 48 * half
                block = image[pl.ds(pl.multiple_of(source * OWN_ROWS, 16), OWN_ROWS), :]
                image_high[at : at + 48, :], image_low[at : at + 48, :] = split(block)

    def multiply(batch):
        span = slice(384 * batch, 384 * batch + 384)
        left = rows_turned[:, span]
        return dot(left, image_high[span, :]) + dot(left, image_low[span, :])

    split_image(0)
    split_image(1)
    for half in range(2):
        for dz in (3, -3):
            rows_landed(half * N_Z + z_at(dz))
        source = half * N_Z + z_at(4)
        landed(row_blocks.at[source, pl.ds(0, CUT)], row_recv.at[source, 0])
        landed(row_blocks.at[source, pl.ds(CUT, BLOCK - CUT)], row_recv.at[source, 1])
    turn_rows(1)
    pairs = multiply(0) + multiply(1)
    total = jnp.zeros((NT, 128), jnp.float32)
    for half in range(2):
        kept = jnp.zeros((NT, BOTH), jnp.float32)
        shared = base[NT * half : NT * half + NT, :]
        for l in range(NL):
            at = PAIRS * half + NT * l
            kept = jnp.where(lane_l == l, pairs[at : at + NT, :], kept)
        high, low = split(kept + shared)
        total = total + dot(high, fold[half]) + dot(low, fold[half])
    share = jnp.sum(jnp.where(band_lanes, total, 0.0), axis=0, keepdims=True)

    part_a[bulk] = share

    def others(number, own, step):
        repeat(0, number - 1, lambda k: step(jnp.where(k < own, k, k + 1)))

    others(BULK, bulk, lambda to: send(part_a.at[bulk], a_send, a_recv, to, wide))
    landed(parcels.at[pl.ds(0, 15)], parcel_send)
    landed(row_blocks.at[pl.ds(0, 15)], row_send)
    landed(part_a.at[pl.ds(0, BULK - 1)], a_recv)
    part_b[wide] = jnp.sum(part_a[...], axis=0)
    in_order = z * 2 + x_hi
    others(WIDE, in_order, lambda to: send(part_b.at[wide], b_send, b_recv, bulk, lax.rem(to, 2) * N_Z + lax.div(to, 2)))
    landed(part_a.at[pl.ds(0, BULK - 1)], a_send)
    landed(part_b.at[pl.ds(0, WIDE - 1)], b_recv)
    result = jnp.where(band_lanes, jnp.sum(part_b[...], axis=0), 0.0)
    lanes = iota((NT, 128), 1)
    for part in range(2):
        value = jnp.where(lax.div(lanes, 64) == part, result, 0.0)
        for shift in (8, 16, 32, 64):
            value = value + pltpu.roll(value, shift, 1)
        out_ref[part] = value[:, 0:NT]
    landed(part_b.at[pl.ds(0, WIDE - 1)], b_send)


def local(eps_corr, pair_rows, pair_cols, coulomb, wing_row, wing_col, pair_head, head_value, head_coulomb, inner_bands):
    bf16, f32 = jnp.bfloat16, jnp.float32
    dma = pltpu.SemaphoreType.DMA
    return pl.pallas_call(
        kernel,
        out_shape=jax.ShapeDtypeStruct((2, NT, NT), f32),
        in_specs=[pl.BlockSpec(memory_space=pltpu.HBM)] * 10,
        out_specs=pl.BlockSpec(memory_space=pltpu.VMEM),
        scratch_shapes=[
            pltpu.VMEM((UNITS, 2, ROWS, UNIT), bf16),
            pltpu.VMEM((2, OWN_ROWS, PAIRS), bf16),
            pltpu.VMEM((2, PAIRS, OWN), bf16),
            pltpu.VMEM((1, OWN), f32),
            pltpu.VMEM((2, OWN), bf16),
            pltpu.VMEM((2, OWN_ROWS), bf16),
            pltpu.VMEM((2, PAIRS), f32),
            pltpu.SMEM((2,), f32),
            pltpu.SMEM((1,), f32),
            pltpu.SMEM((NL,), jnp.int32),
            pltpu.VMEM((BULK, 288, 128), bf16),
            pltpu.VMEM((BOTH, OWN), bf16),
            pltpu.VMEM((WIDE, BLOCK, 128), bf16),
            pltpu.VMEM((ROWS, 256), bf16),
            pltpu.VMEM((BOTH, ROWS), bf16),
            pltpu.VMEM((BOTH, BOTH), bf16),
            pltpu.VMEM((2, BOTH, 128), bf16),
            pltpu.VMEM((ROWS, BOTH), f32),
            pltpu.VMEM((ROWS, BOTH), bf16),
            pltpu.VMEM((ROWS, BOTH), bf16),
            pltpu.VMEM((2 * NT, BOTH), f32),
            pltpu.VMEM((16, 1, 128), f32),
            pltpu.VMEM((16, 1, 128), f32),
            dma((UNITS,)),
            dma((9,)),
            dma,
            dma((BULK,)),
            dma,
            dma((WIDE, 2)),
            dma,
            dma,
            dma,
            dma,
        ],
        compiler_params=pltpu.CompilerParams(
            collective_id=0, has_side_effects=True, vmem_limit_bytes=63 * 1024 * 1024
        ),
    )(
        eps_corr,
        jnp.swapaxes(pair_rows, 1, 2),
        pair_cols,
        coulomb.reshape(1, OWN),
        wing_row,
        wing_col,
        pair_head,
        head_value,
        head_coulomb,
        inner_bands,
    )


def solution(mesh):
    placed = (
        P(None, "bulk", "wide"),
        P(None, None, ("bulk", "wide")),
        P(None, None, ("wide", "bulk")),
        P(("wide", "bulk")),
        P(None, ("wide", "bulk")),
        P(None, ("bulk", "wide")),
        P(),
        P(),
        P(),
        P(),
    )
    return jax.shard_map(local, mesh=mesh, in_specs=placed, out_specs=P(), check_vma=False)
```

```python
import jax
import jax.numpy as jnp
from jax import lax
from jax.experimental import pallas as pl
from jax.experimental.pallas import tpu as pltpu
from jax.sharding import PartitionSpec as P

NT = 8
NL = 12
NVAL = 12
PAIRS = 96
BOTH = 192
ROWS = 768
COLS = 3072
UNITS = 8
UNIT = 384
OWN = 192
OWN_ROWS = 48
N_Z = 8
WIDE = 16
BULK = 16
BLOCK = 80
CUT = 48
STEPS = (0, 1, -1, 2, -2, 3, -3, 4)
HIGHEST = lax.Precision.HIGHEST
MESH = pl.DeviceIdType.MESH
CONTRACT_LAST = (((1,), (1,)), ((), ()))


def dot(a, b, **kw):
    return jnp.dot(a, b, preferred_element_type=jnp.float32, **kw)


def dot_t(a, b, **kw):
    return lax.dot_general(a, b, CONTRACT_LAST, preferred_element_type=jnp.float32, **kw)


def iota(shape, dim):
    return lax.broadcasted_iota(jnp.int32, shape, dim)


def split(value):
    high = value.astype(jnp.bfloat16)
    return high, (value - high.astype(jnp.float32)).astype(jnp.bfloat16)


def kernel(
    eps_hbm,
    rows_hbm,
    cols_hbm,
    coulomb_hbm,
    wing_row_hbm,
    wing_col_hbm,
    head_hbm,
    head_value_hbm,
    head_coulomb_hbm,
    bands_hbm,
    out_ref,
    eps,
    rows,
    cols,
    coulomb,
    wing_row,
    wing_col,
    head,
    head_value_ref,
    head_coulomb_ref,
    bands_ref,
    parcels,
    own_weighted,
    row_blocks,
    rows_stack,
    rows_turned,
    order,
    fold,
    image,
    image_high,
    image_low,
    base,
    part_a,
    part_b,
    eps_sem,
    in_sem,
    parcel_send,
    parcel_recv,
    row_send,
    row_recv,
    a_send,
    a_recv,
    b_send,
    b_recv,
):
    bulk = lax.axis_index("bulk")
    wide = lax.axis_index("wide")
    core = lax.rem(bulk, 2)
    chip = lax.div(bulk, 2)
    x_lo = lax.div(chip, 4)
    y = lax.rem(chip, 4)
    x_hi = lax.div(wide, N_Z)
    z = lax.rem(wide, N_Z)

    def unit_at(dx, dy):
        return lax.rem(x_lo + dx, 2) * 4 + lax.rem(y + dy, 4)

    def unit_of(i):
        return unit_at(lax.div(i, 4), lax.rem(i, 4))

    def z_at(dz):
        return lax.rem(z + dz + N_Z, N_Z)

    here, across = unit_at(0, 0), unit_at(1, 0)

    def repeat(first, last, step):
        def body(i, carry):
            step(i)
            return carry

        lax.fori_loop(first, last, body, 0)

    sibling = chip * 2 + 1 - core
    across_x = lax.rem(x_hi + 1, 2) * N_Z + z

    def along_z(dz):
        return x_hi * N_Z + z_at(dz)

    barrier = pltpu.get_barrier_semaphore()

    def greet(to_bulk, to_wide):
        pl.semaphore_signal(barrier, inc=1, device_id={"bulk": to_bulk, "wide": to_wide}, device_id_type=MESH)

    greet(bulk, across_x)
    greet(sibling, wide)
    greet(across * 2 + core, wide)
    for dy in (1, 3, 2):
        greet(unit_at(0, dy) * 2 + core, wide)
    for dz in (1, -1, 2, -2):
        greet(bulk, along_z(dz))

    small = [
        pltpu.make_async_copy(src, dst, in_sem.at[i])
        for i, (src, dst) in enumerate(
            (
                (rows_hbm, rows),
                (cols_hbm, cols),
                (coulomb_hbm, coulomb),
                (head_hbm, head),
                (wing_row_hbm, wing_row),
                (wing_col_hbm, wing_col),
                (head_value_hbm, head_value_ref),
                (head_coulomb_hbm, head_coulomb_ref),
                (bands_hbm, bands_ref),
            )
        )
    ]
    for copy in small[:3]:
        copy.start()

    def slab(i):
        span = pl.ds(pl.multiple_of(unit_of(i) * UNIT, 128), UNIT)
        return pltpu.make_async_copy(eps_hbm.at[:, :, span], eps.at[i], eps_sem.at[i])

    repeat(0, UNITS, lambda i: slab(i).start())
    for copy in small[3:]:
        copy.start()

    pl.semaphore_wait(barrier, 10)

    def send(place, send_sem, recv_sem, to_bulk, to_wide):
        pltpu.make_async_remote_copy(
            src_ref=place,
            dst_ref=place,
            send_sem=send_sem,
            recv_sem=recv_sem,
            device_id={"bulk": to_bulk, "wide": to_wide},
            device_id_type=MESH,
        ).start()

    def landed(place, sem):
        pltpu.make_async_copy(place, place, sem).wait()

    def send_parcel(of_bulk, to_bulk):
        send(parcels.at[of_bulk], parcel_send, parcel_recv.at[of_bulk], to_bulk, wide)

    def arrived(unit, of_core):
        at = unit * 2 + of_core
        landed(parcels.at[at], parcel_recv.at[at])

    def hand_on(unit):
        send_parcel(unit * 2 + core, sibling)

    def relay(unit, to_chip):
        send_parcel(unit * 2 + core, to_chip * 2 + core)

    def send_rows(of_wide, to_wide):
        send(row_blocks.at[of_wide], row_send, row_recv.at[of_wide, 0], bulk, to_wide)

    def rows_landed(of_wide):
        landed(row_blocks.at[of_wide], row_recv.at[of_wide, 0])

    small[0].wait()
    rows_f32 = rows[...].astype(jnp.float32)
    rows_own = jnp.concatenate([rows_f32[0], rows_f32[1]], axis=1)
    mine_rows = row_blocks.at[wide]
    rows_low = rows_own.astype(jnp.bfloat16)
    mine_rows[0:48] = rows_low[:, :128]
    packed = jnp.concatenate([rows_own[0:24, 128:], rows_own[24:48, 128:]], axis=1)
    mine_rows[48:80] = jnp.concatenate([packed, jnp.zeros((8, 128), jnp.float32)], axis=0).astype(jnp.bfloat16)
    send_rows(wide, across_x)
    small[1].wait()
    small[2].wait()
    weighted = coulomb[...][None] * cols[...].astype(jnp.float32)
    weighted_pairs = weighted.reshape(BOTH, OWN)
    first = core == 0
    main = jnp.where(first, weighted_pairs[:, 0:128], weighted_pairs[:, 64:192])
    near = jnp.where(first, weighted[0][:, 128:192], weighted[1][:, 0:64])
    far = jnp.where(first, weighted[1][:, 128:192], weighted[0][:, 0:64])
    mine = parcels.at[bulk]
    mine[0:192, :] = main.astype(jnp.bfloat16)
    own_weighted[...] = weighted_pairs.astype(jnp.bfloat16)
    mine[192:288, :] = jnp.concatenate([near, far], axis=1).astype(jnp.bfloat16)


    relay(here, across)

    def send_along(of_wide):
        def step(i):
            send_rows(of_wide, along_z(jnp.where(i < 2, i - 2, i - 1)))

        repeat(0, 4, step)

    send_along(wide)
    repeat(1, 4, lambda dy: relay(here, unit_at(0, dy)))
    hand_on(here)

    low_lanes = iota((PAIRS, 128), 1) < 64

    for copy in small[3:]:
        copy.wait()
    pair_re = head[0:1, :]
    pair_im = head[1:2, :]
    head_row = jnp.concatenate([pair_re, pair_im], axis=1)
    turned_row = jnp.concatenate([-pair_im, pair_re], axis=1)
    coulomb_zero = head_coulomb_ref[0]
    scaled_row = coulomb_zero * head_row
    scaled_turned = coulomb_zero * turned_row
    weighted_low = own_weighted[...]
    weighted_turned = jnp.concatenate([-weighted_low[PAIRS:], weighted_low[:PAIRS]], axis=0)
    wing_cols = wing_row[...]
    gain = dot_t(wing_cols, weighted_low)[0:1] + dot_t(wing_cols, weighted_turned)[1:2]
    tilt = dot(wing_col[...], rows_low)
    leads = jnp.where(jnp.logical_and(bulk == 0, wide == 0), 1.0, 0.0)
    from_head = gain + leads * (head_value_ref[0] * scaled_row + head_value_ref[1] * scaled_turned)
    lane = iota((1, BOTH), 1)
    lane_l = lax.rem(lane, NL)
    lane_band = lax.div(lane, NL)
    weight_row = jnp.zeros((1, BOTH), jnp.float32)
    for l in range(NL):
        weight_row = jnp.where(lane_l == l, jnp.where(bands_ref[l] < NVAL, -0.5, 0.5), weight_row)
    row_at = iota((BOTH, 1), 0)
    same_l = jnp.where(lax.rem(row_at, NL) == lane_l, weight_row, 0.0).astype(jnp.bfloat16)
    in_band = iota((2 * NT, BOTH), 0) == lane_band

    def gathered(row):
        spread = jnp.where(in_band, row, 0.0)
        high = spread.astype(jnp.bfloat16)
        middle, low = split(spread - high.astype(jnp.float32))
        return dot(high, same_l) + dot(middle, same_l) + dot(low, same_l)

    base[...] = (
        gathered(head_row) * from_head + gathered(tilt[0:1]) * scaled_row + gathered(tilt[1:2]) * scaled_turned
    )

    to_lane = iota((1, 128), 1)
    low_part = to_lane < 64
    key = jnp.where(low_part, 0, NT) + lax.rem(to_lane, NT)
    row_band = lax.div(row_at, NL)
    fold[0] = jnp.where(row_band == key, 1.0, 0.0).astype(jnp.bfloat16)
    sign = jnp.where(low_part, 1.0, -1.0)
    fold[1] = jnp.where(row_band == jnp.where(low_part, key + NT, key - NT), sign, 0.0).astype(jnp.bfloat16)
    band_lanes = lax.rem(lax.div(to_lane, NT), NT) == iota((NT, 128), 0)
    lane_half = lax.div(lane, PAIRS)
    place = lane_half * PAIRS + lane_l * NT + lane_band - lane_half * NT
    order[...] = jnp.where(iota((BOTH, BOTH), 0) == place, weight_row, 0.0).astype(jnp.bfloat16)
    image[...] = jnp.zeros((ROWS, BOTH), jnp.float32)

    rows_landed(across_x)
    send_along(across_x)

    @pl.when(core == 0)
    def _():
        arrived(across, core)
        repeat(1, 4, lambda dy: relay(across, unit_at(0, dy)))

    @pl.when(core == 1)
    def _():
        for dy in (1, 3):
            arrived(unit_at(0, dy), core)
            relay(unit_at(0, dy), across)
        arrived(across, core)

    hand_on(across)

    def work(i):
        unit = unit_of(i)
        arrived(unit, 1 - core)
        slab(i).wait()
        head_block = parcels[unit * 2, 0:192, :]
        tail_block = parcels[unit * 2 + 1, 0:192, :]
        half0 = parcels[unit * 2, 192:288, :]
        half1 = parcels[unit * 2 + 1, 192:288, :]
        mid_re = jnp.where(low_lanes, half0, half1)
        mid_im = jnp.where(low_lanes, half1, half0)
        mid_im = jnp.concatenate([mid_im[:, 64:], mid_im[:, :64]], axis=1)
        middle = jnp.concatenate([mid_re, mid_im], axis=0)
        plain = jnp.concatenate([head_block, middle, tail_block], axis=1)
        turned = jnp.concatenate([-plain[PAIRS:], plain[:PAIRS]], axis=0)
        left = jnp.concatenate([eps[i, 0], eps[i, 1]], axis=1)
        image[...] += dot_t(left, jnp.concatenate([plain, turned], axis=1))

    def relay_rows(at_x):
        for i, dz in enumerate((1, -1)):
            source = at_x * N_Z + z_at(-2 * dz)
            rows_landed(source)
            piece = row_blocks.at[source, pl.ds(0, CUT) if dz == 1 else pl.ds(CUT, BLOCK - CUT)]
            send(piece, row_send, row_recv.at[source, i], bulk, along_z(2 * dz))
            send_rows(source, along_z(dz))

    def second_stage():
        @pl.when(core == 0)
        def _():
            for dy in (1, 2, 3):
                arrived(unit_at(0, dy), core)

        @pl.when(core == 1)
        def _():
            arrived(unit_at(0, 2), core)
            relay(unit_at(0, 2), across)

        relay_rows(x_hi)
        repeat(1, 4, lambda dy: hand_on(unit_at(0, dy)))
        relay_rows(lax.rem(x_hi + 1, 2))

    def third_stage():
        def step(dy):
            arrived(unit_at(1, dy), core)
            hand_on(unit_at(1, dy))

        repeat(1, 4, step)

    def turn_rows(batch):
        for j in range(4 * batch, 4 * batch + 4):
            for half in range(2):
                source = half * N_Z + z_at(STEPS[j])
                at = 96 * j + 48 * half
                packed = row_blocks[source, 48:72, :].astype(jnp.float32)
                rest = jnp.concatenate([packed, pltpu.roll(packed, 64, 1)], axis=0)
                rows_stack[at : at + 48, 0:128] = row_blocks[source, 0:48, :]
                rows_stack[at : at + 48, 128:256] = rest.astype(jnp.bfloat16)
        span = slice(384 * batch, 384 * batch + 384)
        rows_turned[:, span] = dot_t(order[...], rows_stack[span, 0:BOTH]).astype(jnp.bfloat16)

    def units_step(i):
        @pl.when(i == 1)
        def _():
            second_stage()

        @pl.when(i == 3)
        def _():
            third_stage()

        work(i)

    repeat(0, UNITS, units_step)

    for dz in (1, -1):
        for half in range(2):
            rows_landed(half * N_Z + z_at(dz))
    turn_rows(0)

    def split_image(batch):
        for j in range(4 * batch, 4 * batch + 4):
            for half in range(2):
                source = half * N_Z + z_at(STEPS[j])
                at = 96 * j + 48 * half
                block = image[pl.ds(pl.multiple_of(source * OWN_ROWS, 16), OWN_ROWS), :]
                image_high[at : at + 48, :], image_low[at : at + 48, :] = split(block)

    def multiply(batch):
        span = slice(384 * batch, 384 * batch + 384)
        left = rows_turned[:, span]
        return dot(left, image_high[span, :]) + dot(left, image_low[span, :])

    split_image(0)
    split_image(1)
    for half in range(2):
        for dz in (3, -3):
            rows_landed(half * N_Z + z_at(dz))
        source = half * N_Z + z_at(4)
        landed(row_blocks.at[source, pl.ds(0, CUT)], row_recv.at[source, 0])
        landed(row_blocks.at[source, pl.ds(CUT, BLOCK - CUT)], row_recv.at[source, 1])
    turn_rows(1)
    pairs = multiply(0) + multiply(1)
    total = jnp.zeros((NT, 128), jnp.float32)
    for half in range(2):
        kept = jnp.zeros((NT, BOTH), jnp.float32)
        shared = base[NT * half : NT * half + NT, :]
        for l in range(NL):
            at = PAIRS * half + NT * l
            kept = jnp.where(lane_l == l, pairs[at : at + NT, :], kept)
        high, low = split(kept + shared)
        total = total + dot(high, fold[half]) + dot(low, fold[half])
    share = jnp.sum(jnp.where(band_lanes, total, 0.0), axis=0, keepdims=True)

    part_a[bulk] = share

    def others(number, own, step):
        repeat(0, number - 1, lambda k: step(jnp.where(k < own, k, k + 1)))

    others(BULK, bulk, lambda to: send(part_a.at[bulk], a_send, a_recv, to, wide))
    landed(part_a.at[pl.ds(0, BULK - 1)], a_recv)
    part_b[wide] = jnp.sum(part_a[...], axis=0)
    in_order = z * 2 + x_hi
    others(WIDE, in_order, lambda to: send(part_b.at[wide], b_send, b_recv, bulk, lax.rem(to, 2) * N_Z + lax.div(to, 2)))
    landed(parcels.at[pl.ds(0, 15)], parcel_send)
    landed(row_blocks.at[pl.ds(0, 15)], row_send)
    landed(part_a.at[pl.ds(0, BULK - 1)], a_send)
    landed(part_b.at[pl.ds(0, WIDE - 1)], b_recv)
    result = jnp.where(band_lanes, jnp.sum(part_b[...], axis=0), 0.0)
    lanes = iota((NT, 128), 1)
    for part in range(2):
        value = jnp.where(lax.div(lanes, 64) == part, result, 0.0)
        for shift in (8, 16, 32, 64):
            value = value + pltpu.roll(value, shift, 1)
        out_ref[part] = value[:, 0:NT]
    landed(part_b.at[pl.ds(0, WIDE - 1)], b_send)


def local(eps_corr, pair_rows, pair_cols, coulomb, wing_row, wing_col, pair_head, head_value, head_coulomb, inner_bands):
    bf16, f32 = jnp.bfloat16, jnp.float32
    dma = pltpu.SemaphoreType.DMA
    return pl.pallas_call(
        kernel,
        out_shape=jax.ShapeDtypeStruct((2, NT, NT), f32),
        in_specs=[pl.BlockSpec(memory_space=pltpu.HBM)] * 10,
        out_specs=pl.BlockSpec(memory_space=pltpu.VMEM),
        scratch_shapes=[
            pltpu.VMEM((UNITS, 2, ROWS, UNIT), bf16),
            pltpu.VMEM((2, OWN_ROWS, PAIRS), bf16),
            pltpu.VMEM((2, PAIRS, OWN), bf16),
            pltpu.VMEM((1, OWN), f32),
            pltpu.VMEM((2, OWN), bf16),
            pltpu.VMEM((2, OWN_ROWS), bf16),
            pltpu.VMEM((2, PAIRS), f32),
            pltpu.SMEM((2,), f32),
            pltpu.SMEM((1,), f32),
            pltpu.SMEM((NL,), jnp.int32),
            pltpu.VMEM((BULK, 288, 128), bf16),
            pltpu.VMEM((BOTH, OWN), bf16),
            pltpu.VMEM((WIDE, BLOCK, 128), bf16),
            pltpu.VMEM((ROWS, 256), bf16),
            pltpu.VMEM((BOTH, ROWS), bf16),
            pltpu.VMEM((BOTH, BOTH), bf16),
            pltpu.VMEM((2, BOTH, 128), bf16),
            pltpu.VMEM((ROWS, BOTH), f32),
            pltpu.VMEM((ROWS, BOTH), bf16),
            pltpu.VMEM((ROWS, BOTH), bf16),
            pltpu.VMEM((2 * NT, BOTH), f32),
            pltpu.VMEM((16, 1, 128), f32),
            pltpu.VMEM((16, 1, 128), f32),
            dma((UNITS,)),
            dma((9,)),
            dma,
            dma((BULK,)),
            dma,
            dma((WIDE, 2)),
            dma,
            dma,
            dma,
            dma,
        ],
        compiler_params=pltpu.CompilerParams(
            collective_id=0, has_side_effects=True, vmem_limit_bytes=63 * 1024 * 1024
        ),
    )(
        eps_corr,
        jnp.swapaxes(pair_rows, 1, 2),
        pair_cols,
        coulomb.reshape(1, OWN),
        wing_row,
        wing_col,
        pair_head,
        head_value,
        head_coulomb,
        inner_bands,
    )


def solution(mesh):
    placed = (
        P(None, "bulk", "wide"),
        P(None, None, ("bulk", "wide")),
        P(None, None, ("wide", "bulk")),
        P(("wide", "bulk")),
        P(None, ("wide", "bulk")),
        P(None, ("bulk", "wide")),
        P(),
        P(),
        P(),
        P(),
    )
    return jax.shard_map(local, mesh=mesh, in_specs=placed, out_specs=P(), check_vma=False)
```

```python
import jax
import jax.numpy as jnp
from jax import lax
from jax.experimental import pallas as pl
from jax.experimental.pallas import tpu as pltpu
from jax.sharding import PartitionSpec as P

NT = 8
NL = 12
NVAL = 12
PAIRS = 96
BOTH = 192
ROWS = 768
COLS = 3072
UNITS = 8
UNIT = 384
OWN = 192
OWN_ROWS = 48
N_Z = 8
WIDE = 16
BULK = 16
BLOCK = 80
CUT = 48
STEPS = (0, 1, -1, 2, -2, 3, -3, 4)
HIGHEST = lax.Precision.HIGHEST
MESH = pl.DeviceIdType.MESH
CONTRACT_LAST = (((1,), (1,)), ((), ()))


def dot(a, b, **kw):
    return jnp.dot(a, b, preferred_element_type=jnp.float32, **kw)


def dot_t(a, b, **kw):
    return lax.dot_general(a, b, CONTRACT_LAST, preferred_element_type=jnp.float32, **kw)


def iota(shape, dim):
    return lax.broadcasted_iota(jnp.int32, shape, dim)


def split(value):
    high = value.astype(jnp.bfloat16)
    return high, (value - high.astype(jnp.float32)).astype(jnp.bfloat16)


def kernel(
    eps_hbm,
    rows_hbm,
    cols_hbm,
    coulomb_hbm,
    wing_row_hbm,
    wing_col_hbm,
    head_hbm,
    head_value_hbm,
    head_coulomb_hbm,
    bands_hbm,
    out_ref,
    eps,
    rows,
    cols,
    coulomb,
    wing_row,
    wing_col,
    head,
    head_value_ref,
    head_coulomb_ref,
    bands_ref,
    parcels,
    own_weighted,
    row_blocks,
    rows_stack,
    rows_turned,
    order,
    fold,
    image,
    image_high,
    image_low,
    base,
    part_a,
    part_b,
    eps_sem,
    in_sem,
    parcel_send,
    parcel_recv,
    row_send,
    row_recv,
    a_send,
    a_recv,
    b_send,
    b_recv,
):
    bulk = lax.axis_index("bulk")
    wide = lax.axis_index("wide")
    core = lax.rem(bulk, 2)
    chip = lax.div(bulk, 2)
    x_lo = lax.div(chip, 4)
    y = lax.rem(chip, 4)
    x_hi = lax.div(wide, N_Z)
    z = lax.rem(wide, N_Z)

    def unit_at(dx, dy):
        return lax.rem(x_lo + dx, 2) * 4 + lax.rem(y + dy, 4)

    def unit_of(i):
        return unit_at(lax.div(i, 4), lax.rem(i, 4))

    def z_at(dz):
        return lax.rem(z + dz + N_Z, N_Z)

    here, across = unit_at(0, 0), unit_at(1, 0)

    def repeat(first, last, step):
        def body(i, carry):
            step(i)
            return carry

        if last - first > 4:
            lax.fori_loop(first, last, body, 0)
        else:
            for i in range(first, last):
                step(i)

    sibling = chip * 2 + 1 - core
    across_x = lax.rem(x_hi + 1, 2) * N_Z + z

    def along_z(dz):
        return x_hi * N_Z + z_at(dz)

    barrier = pltpu.get_barrier_semaphore()

    def greet(to_bulk, to_wide):
        pl.semaphore_signal(barrier, inc=1, device_id={"bulk": to_bulk, "wide": to_wide}, device_id_type=MESH)

    greet(bulk, across_x)
    greet(sibling, wide)
    greet(across * 2 + core, wide)
    for dy in (1, 3, 2):
        greet(unit_at(0, dy) * 2 + core, wide)
    for dz in (1, -1, 2, -2):
        greet(bulk, along_z(dz))

    small = [
        pltpu.make_async_copy(src, dst, in_sem.at[i])
        for i, (src, dst) in enumerate(
            (
                (rows_hbm, rows),
                (cols_hbm, cols),
                (coulomb_hbm, coulomb),
                (head_hbm, head),
                (wing_row_hbm, wing_row),
                (wing_col_hbm, wing_col),
                (head_value_hbm, head_value_ref),
                (head_coulomb_hbm, head_coulomb_ref),
                (bands_hbm, bands_ref),
            )
        )
    ]
    for copy in small[:3]:
        copy.start()

    def slab(i):
        span = pl.ds(pl.multiple_of(unit_of(i) * UNIT, 128), UNIT)
        return pltpu.make_async_copy(eps_hbm.at[:, :, span], eps.at[i], eps_sem.at[i])

    repeat(0, UNITS, lambda i: slab(i).start())
    for copy in small[3:]:
        copy.start()

    pl.semaphore_wait(barrier, 10)

    def send(place, send_sem, recv_sem, to_bulk, to_wide):
        pltpu.make_async_remote_copy(
            src_ref=place,
            dst_ref=place,
            send_sem=send_sem,
            recv_sem=recv_sem,
            device_id={"bulk": to_bulk, "wide": to_wide},
            device_id_type=MESH,
        ).start()

    def landed(place, sem):
        pltpu.make_async_copy(place, place, sem).wait()

    def send_parcel(of_bulk, to_bulk):
        send(parcels.at[of_bulk], parcel_send, parcel_recv.at[of_bulk], to_bulk, wide)

    def arrived(unit, of_core):
        at = unit * 2 + of_core
        landed(parcels.at[at], parcel_recv.at[at])

    def hand_on(unit):
        send_parcel(unit * 2 + core, sibling)

    def relay(unit, to_chip):
        send_parcel(unit * 2 + core, to_chip * 2 + core)

    def send_rows(of_wide, to_wide):
        send(row_blocks.at[of_wide], row_send, row_recv.at[of_wide, 0], bulk, to_wide)

    def rows_landed(of_wide):
        landed(row_blocks.at[of_wide], row_recv.at[of_wide, 0])

    small[0].wait()
    rows_f32 = rows[...].astype(jnp.float32)
    rows_own = jnp.concatenate([rows_f32[0], rows_f32[1]], axis=1)
    mine_rows = row_blocks.at[wide]
    rows_low = rows_own.astype(jnp.bfloat16)
    mine_rows[0:48] = rows_low[:, :128]
    packed = jnp.concatenate([rows_own[0:24, 128:], rows_own[24:48, 128:]], axis=1)
    mine_rows[48:80] = jnp.concatenate([packed, jnp.zeros((8, 128), jnp.float32)], axis=0).astype(jnp.bfloat16)
    send_rows(wide, across_x)
    small[1].wait()
    small[2].wait()
    weighted = coulomb[...][None] * cols[...].astype(jnp.float32)
    weighted_pairs = weighted.reshape(BOTH, OWN)
    first = core == 0
    main = jnp.where(first, weighted_pairs[:, 0:128], weighted_pairs[:, 64:192])
    near = jnp.where(first, weighted[0][:, 128:192], weighted[1][:, 0:64])
    far = jnp.where(first, weighted[1][:, 128:192], weighted[0][:, 0:64])
    mine = parcels.at[bulk]
    mine[0:192, :] = main.astype(jnp.bfloat16)
    own_weighted[...] = weighted_pairs.astype(jnp.bfloat16)
    mine[192:288, :] = jnp.concatenate([near, far], axis=1).astype(jnp.bfloat16)


    relay(here, across)

    def send_along(of_wide):
        def step(i):
            send_rows(of_wide, along_z((2, -2, 1, -1)[i]))

        repeat(0, 4, step)

    send_along(wide)
    repeat(1, 4, lambda dy: relay(here, unit_at(0, dy)))
    hand_on(here)

    low_lanes = iota((PAIRS, 128), 1) < 64

    for copy in small[3:]:
        copy.wait()
    pair_re = head[0:1, :]
    pair_im = head[1:2, :]
    head_row = jnp.concatenate([pair_re, pair_im], axis=1)
    turned_row = jnp.concatenate([-pair_im, pair_re], axis=1)
    coulomb_zero = head_coulomb_ref[0]
    scaled_row = coulomb_zero * head_row
    scaled_turned = coulomb_zero * turned_row
    weighted_low = own_weighted[...]
    weighted_turned = jnp.concatenate([-weighted_low[PAIRS:], weighted_low[:PAIRS]], axis=0)
    wing_cols = wing_row[...]
    gain = dot_t(wing_cols, weighted_low)[0:1] + dot_t(wing_cols, weighted_turned)[1:2]
    tilt = dot(wing_col[...], rows_low)
    leads = jnp.where(jnp.logical_and(bulk == 0, wide == 0), 1.0, 0.0)
    from_head = gain + leads * (head_value_ref[0] * scaled_row + head_value_ref[1] * scaled_turned)
    lane = iota((1, BOTH), 1)
    lane_l = lax.rem(lane, NL)
    lane_band = lax.div(lane, NL)
    weight_row = jnp.zeros((1, BOTH), jnp.float32)
    for l in range(NL):
        weight_row = jnp.where(lane_l == l, jnp.where(bands_ref[l] < NVAL, -0.5, 0.5), weight_row)
    row_at = iota((BOTH, 1), 0)
    same_l = jnp.where(lax.rem(row_at, NL) == lane_l, weight_row, 0.0).astype(jnp.bfloat16)
    in_band = iota((2 * NT, BOTH), 0) == lane_band

    def gathered(row):
        spread = jnp.where(in_band, row, 0.0)
        high = spread.astype(jnp.bfloat16)
        middle, low = split(spread - high.astype(jnp.float32))
        return dot(high, same_l) + dot(middle, same_l) + dot(low, same_l)

    base[...] = (
        gathered(head_row) * from_head + gathered(tilt[0:1]) * scaled_row + gathered(tilt[1:2]) * scaled_turned
    )

    to_lane = iota((1, 128), 1)
    low_part = to_lane < 64
    key = jnp.where(low_part, 0, NT) + lax.rem(to_lane, NT)
    row_band = lax.div(row_at, NL)
    fold[0] = jnp.where(row_band == key, 1.0, 0.0).astype(jnp.bfloat16)
    sign = jnp.where(low_part, 1.0, -1.0)
    fold[1] = jnp.where(row_band == jnp.where(low_part, key + NT, key - NT), sign, 0.0).astype(jnp.bfloat16)
    band_lanes = lax.rem(lax.div(to_lane, NT), NT) == iota((NT, 128), 0)
    lane_half = lax.div(lane, PAIRS)
    place = lane_half * PAIRS + lane_l * NT + lane_band - lane_half * NT
    order[...] = jnp.where(iota((BOTH, BOTH), 0) == place, weight_row, 0.0).astype(jnp.bfloat16)
    image[...] = jnp.zeros((ROWS, BOTH), jnp.float32)

    rows_landed(across_x)
    send_along(across_x)

    @pl.when(core == 0)
    def _():
        arrived(across, core)
        repeat(1, 4, lambda dy: relay(across, unit_at(0, dy)))

    @pl.when(core == 1)
    def _():
        for dy in (1, 3):
            arrived(unit_at(0, dy), core)
            relay(unit_at(0, dy), across)
        arrived(across, core)

    hand_on(across)

    def work(i):
        unit = unit_of(i)
        arrived(unit, 1 - core)
        slab(i).wait()
        head_block = parcels[unit * 2, 0:192, :]
        tail_block = parcels[unit * 2 + 1, 0:192, :]
        half0 = parcels[unit * 2, 192:288, :]
        half1 = parcels[unit * 2 + 1, 192:288, :]
        mid_re = jnp.where(low_lanes, half0, half1)
        mid_im = jnp.where(low_lanes, half1, half0)
        mid_im = jnp.concatenate([mid_im[:, 64:], mid_im[:, :64]], axis=1)
        middle = jnp.concatenate([mid_re, mid_im], axis=0)
        plain = jnp.concatenate([head_block, middle, tail_block], axis=1)
        turned = jnp.concatenate([-plain[PAIRS:], plain[:PAIRS]], axis=0)
        left = jnp.concatenate([eps[i, 0], eps[i, 1]], axis=1)
        image[...] += dot_t(left, jnp.concatenate([plain, turned], axis=1))

    def relay_rows(at_x):
        for i, dz in enumerate((1, -1)):
            source = at_x * N_Z + z_at(-2 * dz)
            rows_landed(source)
            piece = row_blocks.at[source, pl.ds(0, CUT) if dz == 1 else pl.ds(CUT, BLOCK - CUT)]
            send(piece, row_send, row_recv.at[source, i], bulk, along_z(2 * dz))
            send_rows(source, along_z(dz))

    def second_stage():
        @pl.when(core == 0)
        def _():
            for dy in (1, 2, 3):
                arrived(unit_at(0, dy), core)

        @pl.when(core == 1)
        def _():
            arrived(unit_at(0, 2), core)
            relay(unit_at(0, 2), across)

        relay_rows(x_hi)
        repeat(1, 4, lambda dy: hand_on(unit_at(0, dy)))
        relay_rows(lax.rem(x_hi + 1, 2))

    def third_stage():
        def step(dy):
            arrived(unit_at(1, dy), core)
            hand_on(unit_at(1, dy))

        repeat(1, 4, step)

    def turn_rows(batch):
        for j in range(4 * batch, 4 * batch + 4):
            for half in range(2):
                source = half * N_Z + z_at(STEPS[j])
                at = 96 * j + 48 * half
                packed = row_blocks[source, 48:72, :].astype(jnp.float32)
                rest = jnp.concatenate([packed, pltpu.roll(packed, 64, 1)], axis=0)
                rows_stack[at : at + 48, 0:128] = row_blocks[source, 0:48, :]
                rows_stack[at : at + 48, 128:256] = rest.astype(jnp.bfloat16)
        span = slice(384 * batch, 384 * batch + 384)
        rows_turned[:, span] = dot_t(order[...], rows_stack[span, 0:BOTH]).astype(jnp.bfloat16)

    def units_step(i):
        @pl.when(i == 1)
        def _():
            second_stage()

        @pl.when(i == 3)
        def _():
            third_stage()

        work(i)

    repeat(0, UNITS, units_step)

    for dz in (1, -1):
        for half in range(2):
            rows_landed(half * N_Z + z_at(dz))
    turn_rows(0)

    def split_image(batch):
        for j in range(4 * batch, 4 * batch + 4):
            for half in range(2):
                source = half * N_Z + z_at(STEPS[j])
                at = 96 * j + 48 * half
                block = image[pl.ds(pl.multiple_of(source * OWN_ROWS, 16), OWN_ROWS), :]
                image_high[at : at + 48, :], image_low[at : at + 48, :] = split(block)

    def multiply(batch):
        span = slice(384 * batch, 384 * batch + 384)
        left = rows_turned[:, span]
        return dot(left, image_high[span, :]) + dot(left, image_low[span, :])

    split_image(0)
    split_image(1)
    for half in range(2):
        for dz in (3, -3):
            rows_landed(half * N_Z + z_at(dz))
        source = half * N_Z + z_at(4)
        landed(row_blocks.at[source, pl.ds(0, CUT)], row_recv.at[source, 0])
        landed(row_blocks.at[source, pl.ds(CUT, BLOCK - CUT)], row_recv.at[source, 1])
    turn_rows(1)
    pairs = multiply(0) + multiply(1)
    total = jnp.zeros((NT, 128), jnp.float32)
    for half in range(2):
        kept = jnp.zeros((NT, BOTH), jnp.float32)
        shared = base[NT * half : NT * half + NT, :]
        for l in range(NL):
            at = PAIRS * half + NT * l
            kept = jnp.where(lane_l == l, pairs[at : at + NT, :], kept)
        high, low = split(kept + shared)
        total = total + dot(high, fold[half]) + dot(low, fold[half])
    share = jnp.sum(jnp.where(band_lanes, total, 0.0), axis=0, keepdims=True)

    part_a[bulk] = share

    def others(number, own, step):
        repeat(0, number - 1, lambda k: step(jnp.where(k < own, k, k + 1)))

    others(BULK, bulk, lambda to: send(part_a.at[bulk], a_send, a_recv, to, wide))
    landed(part_a.at[pl.ds(0, BULK - 1)], a_recv)
    part_b[wide] = jnp.sum(part_a[...], axis=0)
    in_order = z * 2 + x_hi
    others(WIDE, in_order, lambda to: send(part_b.at[wide], b_send, b_recv, bulk, lax.rem(to, 2) * N_Z + lax.div(to, 2)))
    landed(parcels.at[pl.ds(0, 15)], parcel_send)
    landed(row_blocks.at[pl.ds(0, 15)], row_send)
    landed(part_a.at[pl.ds(0, BULK - 1)], a_send)
    landed(part_b.at[pl.ds(0, WIDE - 1)], b_recv)
    result = jnp.where(band_lanes, jnp.sum(part_b[...], axis=0), 0.0)
    lanes = iota((NT, 128), 1)
    for part in range(2):
        value = jnp.where(lax.div(lanes, 64) == part, result, 0.0)
        for shift in (8, 16, 32, 64):
            value = value + pltpu.roll(value, shift, 1)
        out_ref[part] = value[:, 0:NT]
    landed(part_b.at[pl.ds(0, WIDE - 1)], b_send)


def local(eps_corr, pair_rows, pair_cols, coulomb, wing_row, wing_col, pair_head, head_value, head_coulomb, inner_bands):
    bf16, f32 = jnp.bfloat16, jnp.float32
    dma = pltpu.SemaphoreType.DMA
    return pl.pallas_call(
        kernel,
        out_shape=jax.ShapeDtypeStruct((2, NT, NT), f32),
        in_specs=[pl.BlockSpec(memory_space=pltpu.HBM)] * 10,
        out_specs=pl.BlockSpec(memory_space=pltpu.VMEM),
        scratch_shapes=[
            pltpu.VMEM((UNITS, 2, ROWS, UNIT), bf16),
            pltpu.VMEM((2, OWN_ROWS, PAIRS), bf16),
            pltpu.VMEM((2, PAIRS, OWN), bf16),
            pltpu.VMEM((1, OWN), f32),
            pltpu.VMEM((2, OWN), bf16),
            pltpu.VMEM((2, OWN_ROWS), bf16),
            pltpu.VMEM((2, PAIRS), f32),
            pltpu.SMEM((2,), f32),
            pltpu.SMEM((1,), f32),
            pltpu.SMEM((NL,), jnp.int32),
            pltpu.VMEM((BULK, 288, 128), bf16),
            pltpu.VMEM((BOTH, OWN), bf16),
            pltpu.VMEM((WIDE, BLOCK, 128), bf16),
            pltpu.VMEM((ROWS, 256), bf16),
            pltpu.VMEM((BOTH, ROWS), bf16),
            pltpu.VMEM((BOTH, BOTH), bf16),
            pltpu.VMEM((2, BOTH, 128), bf16),
            pltpu.VMEM((ROWS, BOTH), f32),
            pltpu.VMEM((ROWS, BOTH), bf16),
            pltpu.VMEM((ROWS, BOTH), bf16),
            pltpu.VMEM((2 * NT, BOTH), f32),
            pltpu.VMEM((16, 1, 128), f32),
            pltpu.VMEM((16, 1, 128), f32),
            dma((UNITS,)),
            dma((9,)),
            dma,
            dma((BULK,)),
            dma,
            dma((WIDE, 2)),
            dma,
            dma,
            dma,
            dma,
        ],
        compiler_params=pltpu.CompilerParams(
            collective_id=0, has_side_effects=True, vmem_limit_bytes=63 * 1024 * 1024
        ),
    )(
        eps_corr,
        jnp.swapaxes(pair_rows, 1, 2),
        pair_cols,
        coulomb.reshape(1, OWN),
        wing_row,
        wing_col,
        pair_head,
        head_value,
        head_coulomb,
        inner_bands,
    )


def solution(mesh):
    placed = (
        P(None, "bulk", "wide"),
        P(None, None, ("bulk", "wide")),
        P(None, None, ("wide", "bulk")),
        P(("wide", "bulk")),
        P(None, ("wide", "bulk")),
        P(None, ("bulk", "wide")),
        P(),
        P(),
        P(),
        P(),
    )
    return jax.shard_map(local, mesh=mesh, in_specs=placed, out_specs=P(), check_vma=False)
```

```python
import jax
import jax.numpy as jnp
from jax import lax
from jax.experimental import pallas as pl
from jax.experimental.pallas import tpu as pltpu
from jax.sharding import PartitionSpec as P

NT = 8
NL = 12
NVAL = 12
PAIRS = 96
BOTH = 192
ROWS = 768
COLS = 3072
UNITS = 8
UNIT = 384
OWN = 192
OWN_ROWS = 48
N_Z = 8
WIDE = 16
BULK = 16
BLOCK = 80
CUT = 48
STEPS = (0, 1, -1, 2, -2, 3, -3, 4)
HIGHEST = lax.Precision.HIGHEST
MESH = pl.DeviceIdType.MESH
CONTRACT_LAST = (((1,), (1,)), ((), ()))


def dot(a, b, **kw):
    return jnp.dot(a, b, preferred_element_type=jnp.float32, **kw)


def dot_t(a, b, **kw):
    return lax.dot_general(a, b, CONTRACT_LAST, preferred_element_type=jnp.float32, **kw)


def iota(shape, dim):
    return lax.broadcasted_iota(jnp.int32, shape, dim)


def split(value):
    high = value.astype(jnp.bfloat16)
    return high, (value - high.astype(jnp.float32)).astype(jnp.bfloat16)


def kernel(
    eps_hbm,
    rows_hbm,
    cols_hbm,
    coulomb_hbm,
    wing_row_hbm,
    wing_col_hbm,
    head_hbm,
    head_value_hbm,
    head_coulomb_hbm,
    bands_hbm,
    out_ref,
    eps,
    rows,
    cols,
    coulomb,
    wing_row,
    wing_col,
    head,
    head_value_ref,
    head_coulomb_ref,
    bands_ref,
    parcels,
    own_weighted,
    row_blocks,
    rows_stack,
    rows_turned,
    order,
    fold,
    image,
    image_high,
    image_low,
    base,
    part_a,
    part_b,
    eps_sem,
    in_sem,
    parcel_send,
    parcel_recv,
    row_send,
    row_recv,
    a_send,
    a_recv,
    b_send,
    b_recv,
):
    bulk = lax.axis_index("bulk")
    wide = lax.axis_index("wide")
    core = lax.rem(bulk, 2)
    chip = lax.div(bulk, 2)
    x_lo = lax.div(chip, 4)
    y = lax.rem(chip, 4)
    x_hi = lax.div(wide, N_Z)
    z = lax.rem(wide, N_Z)

    def unit_at(dx, dy):
        return lax.rem(x_lo + dx, 2) * 4 + lax.rem(y + dy, 4)

    def unit_of(i):
        return unit_at(lax.div(i, 4), lax.rem(i, 4))

    def z_at(dz):
        return lax.rem(z + dz + N_Z, N_Z)

    here, across = unit_at(0, 0), unit_at(1, 0)

    def repeat(first, last, step):
        def body(i, carry):
            step(i)
            return carry

        if last - first > 4:
            lax.fori_loop(first, last, body, 0)
        else:
            for i in range(first, last):
                step(i)

    sibling = chip * 2 + 1 - core
    across_x = lax.rem(x_hi + 1, 2) * N_Z + z

    def along_z(dz):
        return x_hi * N_Z + z_at(dz)

    barrier = pltpu.get_barrier_semaphore()

    def greet(to_bulk, to_wide):
        pl.semaphore_signal(barrier, inc=1, device_id={"bulk": to_bulk, "wide": to_wide}, device_id_type=MESH)

    greet(bulk, across_x)
    greet(sibling, wide)
    greet(across * 2 + core, wide)
    for dy in (1, 3, 2):
        greet(unit_at(0, dy) * 2 + core, wide)
    for dz in (1, -1, 2, -2):
        greet(bulk, along_z(dz))

    small = [
        pltpu.make_async_copy(src, dst, in_sem.at[i])
        for i, (src, dst) in enumerate(
            (
                (rows_hbm, rows),
                (cols_hbm, cols),
                (coulomb_hbm, coulomb),
                (head_hbm, head),
                (wing_row_hbm, wing_row),
                (wing_col_hbm, wing_col),
                (head_value_hbm, head_value_ref),
                (head_coulomb_hbm, head_coulomb_ref),
                (bands_hbm, bands_ref),
            )
        )
    ]
    for copy in small[:3]:
        copy.start()

    def slab(i):
        span = pl.ds(pl.multiple_of(unit_of(i) * UNIT, 128), UNIT)
        return pltpu.make_async_copy(eps_hbm.at[:, :, span], eps.at[i], eps_sem.at[i])

    for copy in small[3:]:
        copy.start()

    pl.semaphore_wait(barrier, 10)

    def send(place, send_sem, recv_sem, to_bulk, to_wide):
        pltpu.make_async_remote_copy(
            src_ref=place,
            dst_ref=place,
            send_sem=send_sem,
            recv_sem=recv_sem,
            device_id={"bulk": to_bulk, "wide": to_wide},
            device_id_type=MESH,
        ).start()

    def landed(place, sem):
        pltpu.make_async_copy(place, place, sem).wait()

    def send_parcel(of_bulk, to_bulk):
        send(parcels.at[of_bulk], parcel_send, parcel_recv.at[of_bulk], to_bulk, wide)

    def arrived(unit, of_core):
        at = unit * 2 + of_core
        landed(parcels.at[at], parcel_recv.at[at])

    def hand_on(unit):
        send_parcel(unit * 2 + core, sibling)

    def relay(unit, to_chip):
        send_parcel(unit * 2 + core, to_chip * 2 + core)

    def send_rows(of_wide, to_wide):
        send(row_blocks.at[of_wide], row_send, row_recv.at[of_wide, 0], bulk, to_wide)

    def rows_landed(of_wide):
        landed(row_blocks.at[of_wide], row_recv.at[of_wide, 0])

    small[0].wait()
    rows_f32 = rows[...].astype(jnp.float32)
    rows_own = jnp.concatenate([rows_f32[0], rows_f32[1]], axis=1)
    mine_rows = row_blocks.at[wide]
    rows_low = rows_own.astype(jnp.bfloat16)
    mine_rows[0:48] = rows_low[:, :128]
    packed = jnp.concatenate([rows_own[0:24, 128:], rows_own[24:48, 128:]], axis=1)
    mine_rows[48:80] = jnp.concatenate([packed, jnp.zeros((8, 128), jnp.float32)], axis=0).astype(jnp.bfloat16)
    send_rows(wide, across_x)
    small[1].wait()
    small[2].wait()
    weighted = coulomb[...][None] * cols[...].astype(jnp.float32)
    weighted_pairs = weighted.reshape(BOTH, OWN)
    first = core == 0
    main = jnp.where(first, weighted_pairs[:, 0:128], weighted_pairs[:, 64:192])
    near = jnp.where(first, weighted[0][:, 128:192], weighted[1][:, 0:64])
    far = jnp.where(first, weighted[1][:, 128:192], weighted[0][:, 0:64])
    mine = parcels.at[bulk]
    mine[0:192, :] = main.astype(jnp.bfloat16)
    own_weighted[...] = weighted_pairs.astype(jnp.bfloat16)
    mine[192:288, :] = jnp.concatenate([near, far], axis=1).astype(jnp.bfloat16)


    relay(here, across)

    def send_along(of_wide):
        def step(i):
            send_rows(of_wide, along_z((2, -2, 1, -1)[i]))

        repeat(0, 4, step)

    send_along(wide)
    repeat(1, 4, lambda dy: relay(here, unit_at(0, dy)))
    hand_on(here)
    repeat(0, UNITS, lambda i: slab(i).start())

    low_lanes = iota((PAIRS, 128), 1) < 64

    for copy in small[3:]:
        copy.wait()
    pair_re = head[0:1, :]
    pair_im = head[1:2, :]
    head_row = jnp.concatenate([pair_re, pair_im], axis=1)
    turned_row = jnp.concatenate([-pair_im, pair_re], axis=1)
    coulomb_zero = head_coulomb_ref[0]
    scaled_row = coulomb_zero * head_row
    scaled_turned = coulomb_zero * turned_row
    weighted_low = own_weighted[...]
    weighted_turned = jnp.concatenate([-weighted_low[PAIRS:], weighted_low[:PAIRS]], axis=0)
    wing_cols = wing_row[...]
    gain = dot_t(wing_cols, weighted_low)[0:1] + dot_t(wing_cols, weighted_turned)[1:2]
    tilt = dot(wing_col[...], rows_low)
    leads = jnp.where(jnp.logical_and(bulk == 0, wide == 0), 1.0, 0.0)
    from_head = gain + leads * (head_value_ref[0] * scaled_row + head_value_ref[1] * scaled_turned)
    lane = iota((1, BOTH), 1)
    lane_l = lax.rem(lane, NL)
    lane_band = lax.div(lane, NL)
    weight_row = jnp.zeros((1, BOTH), jnp.float32)
    for l in range(NL):
        weight_row = jnp.where(lane_l == l, jnp.where(bands_ref[l] < NVAL, -0.5, 0.5), weight_row)
    row_at = iota((BOTH, 1), 0)
    same_l = jnp.where(lax.rem(row_at, NL) == lane_l, weight_row, 0.0).astype(jnp.bfloat16)
    in_band = iota((2 * NT, BOTH), 0) == lane_band

    def gathered(row):
        spread = jnp.where(in_band, row, 0.0)
        high = spread.astype(jnp.bfloat16)
        middle, low = split(spread - high.astype(jnp.float32))
        return dot(high, same_l) + dot(middle, same_l) + dot(low, same_l)

    base[...] = (
        gathered(head_row) * from_head + gathered(tilt[0:1]) * scaled_row + gathered(tilt[1:2]) * scaled_turned
    )

    to_lane = iota((1, 128), 1)
    low_part = to_lane < 64
    key = jnp.where(low_part, 0, NT) + lax.rem(to_lane, NT)
    row_band = lax.div(row_at, NL)
    fold[0] = jnp.where(row_band == key, 1.0, 0.0).astype(jnp.bfloat16)
    sign = jnp.where(low_part, 1.0, -1.0)
    fold[1] = jnp.where(row_band == jnp.where(low_part, key + NT, key - NT), sign, 0.0).astype(jnp.bfloat16)
    band_lanes = lax.rem(lax.div(to_lane, NT), NT) == iota((NT, 128), 0)
    lane_half = lax.div(lane, PAIRS)
    place = lane_half * PAIRS + lane_l * NT + lane_band - lane_half * NT
    order[...] = jnp.where(iota((BOTH, BOTH), 0) == place, weight_row, 0.0).astype(jnp.bfloat16)
    image[...] = jnp.zeros((ROWS, BOTH), jnp.float32)

    rows_landed(across_x)
    send_along(across_x)

    @pl.when(core == 0)
    def _():
        arrived(across, core)
        repeat(1, 4, lambda dy: relay(across, unit_at(0, dy)))

    @pl.when(core == 1)
    def _():
        for dy in (1, 3):
            arrived(unit_at(0, dy), core)
            relay(unit_at(0, dy), across)
        arrived(across, core)

    hand_on(across)

    def work(i):
        unit = unit_of(i)
        arrived(unit, 1 - core)
        slab(i).wait()
        head_block = parcels[unit * 2, 0:192, :]
        tail_block = parcels[unit * 2 + 1, 0:192, :]
        half0 = parcels[unit * 2, 192:288, :]
        half1 = parcels[unit * 2 + 1, 192:288, :]
        mid_re = jnp.where(low_lanes, half0, half1)
        mid_im = jnp.where(low_lanes, half1, half0)
        mid_im = jnp.concatenate([mid_im[:, 64:], mid_im[:, :64]], axis=1)
        middle = jnp.concatenate([mid_re, mid_im], axis=0)
        plain = jnp.concatenate([head_block, middle, tail_block], axis=1)
        turned = jnp.concatenate([-plain[PAIRS:], plain[:PAIRS]], axis=0)
        left = jnp.concatenate([eps[i, 0], eps[i, 1]], axis=1)
        image[...] += dot_t(left, jnp.concatenate([plain, turned], axis=1))

    def relay_rows(at_x):
        for i, dz in enumerate((1, -1)):
            source = at_x * N_Z + z_at(-2 * dz)
            rows_landed(source)
            piece = row_blocks.at[source, pl.ds(0, CUT) if dz == 1 else pl.ds(CUT, BLOCK - CUT)]
            send(piece, row_send, row_recv.at[source, i], bulk, along_z(2 * dz))
            send_rows(source, along_z(dz))

    def second_stage():
        @pl.when(core == 0)
        def _():
            for dy in (1, 2, 3):
                arrived(unit_at(0, dy), core)

        @pl.when(core == 1)
        def _():
            arrived(unit_at(0, 2), core)
            relay(unit_at(0, 2), across)

        relay_rows(x_hi)
        repeat(1, 4, lambda dy: hand_on(unit_at(0, dy)))
        relay_rows(lax.rem(x_hi + 1, 2))

    def third_stage():
        def step(dy):
            arrived(unit_at(1, dy), core)
            hand_on(unit_at(1, dy))

        repeat(1, 4, step)

    def turn_rows(batch):
        for j in range(4 * batch, 4 * batch + 4):
            for half in range(2):
                source = half * N_Z + z_at(STEPS[j])
                at = 96 * j + 48 * half
                packed = row_blocks[source, 48:72, :].astype(jnp.float32)
                rest = jnp.concatenate([packed, pltpu.roll(packed, 64, 1)], axis=0)
                rows_stack[at : at + 48, 0:128] = row_blocks[source, 0:48, :]
                rows_stack[at : at + 48, 128:256] = rest.astype(jnp.bfloat16)
        span = slice(384 * batch, 384 * batch + 384)
        rows_turned[:, span] = dot_t(order[...], rows_stack[span, 0:BOTH]).astype(jnp.bfloat16)

    def units_step(i):
        @pl.when(i == 1)
        def _():
            second_stage()

        @pl.when(i == 3)
        def _():
            third_stage()

        work(i)

    repeat(0, UNITS, units_step)

    for dz in (1, -1):
        for half in range(2):
            rows_landed(half * N_Z + z_at(dz))
    turn_rows(0)

    def split_image(batch):
        for j in range(4 * batch, 4 * batch + 4):
            for half in range(2):
                source = half * N_Z + z_at(STEPS[j])
                at = 96 * j + 48 * half
                block = image[pl.ds(pl.multiple_of(source * OWN_ROWS, 16), OWN_ROWS), :]
                image_high[at : at + 48, :], image_low[at : at + 48, :] = split(block)

    def multiply(batch):
        span = slice(384 * batch, 384 * batch + 384)
        left = rows_turned[:, span]
        return dot(left, image_high[span, :]) + dot(left, image_low[span, :])

    split_image(0)
    split_image(1)
    for half in range(2):
        for dz in (3, -3):
            rows_landed(half * N_Z + z_at(dz))
        source = half * N_Z + z_at(4)
        landed(row_blocks.at[source, pl.ds(0, CUT)], row_recv.at[source, 0])
        landed(row_blocks.at[source, pl.ds(CUT, BLOCK - CUT)], row_recv.at[source, 1])
    turn_rows(1)
    pairs = multiply(0) + multiply(1)
    total = jnp.zeros((NT, 128), jnp.float32)
    for half in range(2):
        kept = jnp.zeros((NT, BOTH), jnp.float32)
        shared = base[NT * half : NT * half + NT, :]
        for l in range(NL):
            at = PAIRS * half + NT * l
            kept = jnp.where(lane_l == l, pairs[at : at + NT, :], kept)
        high, low = split(kept + shared)
        total = total + dot(high, fold[half]) + dot(low, fold[half])
    share = jnp.sum(jnp.where(band_lanes, total, 0.0), axis=0, keepdims=True)

    part_a[bulk] = share

    def others(number, own, step):
        repeat(0, number - 1, lambda k: step(jnp.where(k < own, k, k + 1)))

    others(BULK, bulk, lambda to: send(part_a.at[bulk], a_send, a_recv, to, wide))
    landed(part_a.at[pl.ds(0, BULK - 1)], a_recv)
    part_b[wide] = jnp.sum(part_a[...], axis=0)
    in_order = z * 2 + x_hi
    others(WIDE, in_order, lambda to: send(part_b.at[wide], b_send, b_recv, bulk, lax.rem(to, 2) * N_Z + lax.div(to, 2)))
    landed(parcels.at[pl.ds(0, 15)], parcel_send)
    landed(row_blocks.at[pl.ds(0, 15)], row_send)
    landed(part_a.at[pl.ds(0, BULK - 1)], a_send)
    landed(part_b.at[pl.ds(0, WIDE - 1)], b_recv)
    result = jnp.where(band_lanes, jnp.sum(part_b[...], axis=0), 0.0)
    lanes = iota((NT, 128), 1)
    for part in range(2):
        value = jnp.where(lax.div(lanes, 64) == part, result, 0.0)
        for shift in (8, 16, 32, 64):
            value = value + pltpu.roll(value, shift, 1)
        out_ref[part] = value[:, 0:NT]
    landed(part_b.at[pl.ds(0, WIDE - 1)], b_send)


def local(eps_corr, pair_rows, pair_cols, coulomb, wing_row, wing_col, pair_head, head_value, head_coulomb, inner_bands):
    bf16, f32 = jnp.bfloat16, jnp.float32
    dma = pltpu.SemaphoreType.DMA
    return pl.pallas_call(
        kernel,
        out_shape=jax.ShapeDtypeStruct((2, NT, NT), f32),
        in_specs=[pl.BlockSpec(memory_space=pltpu.HBM)] * 10,
        out_specs=pl.BlockSpec(memory_space=pltpu.VMEM),
        scratch_shapes=[
            pltpu.VMEM((UNITS, 2, ROWS, UNIT), bf16),
            pltpu.VMEM((2, OWN_ROWS, PAIRS), bf16),
            pltpu.VMEM((2, PAIRS, OWN), bf16),
            pltpu.VMEM((1, OWN), f32),
            pltpu.VMEM((2, OWN), bf16),
            pltpu.VMEM((2, OWN_ROWS), bf16),
            pltpu.VMEM((2, PAIRS), f32),
            pltpu.SMEM((2,), f32),
            pltpu.SMEM((1,), f32),
            pltpu.SMEM((NL,), jnp.int32),
            pltpu.VMEM((BULK, 288, 128), bf16),
            pltpu.VMEM((BOTH, OWN), bf16),
            pltpu.VMEM((WIDE, BLOCK, 128), bf16),
            pltpu.VMEM((ROWS, 256), bf16),
            pltpu.VMEM((BOTH, ROWS), bf16),
            pltpu.VMEM((BOTH, BOTH), bf16),
            pltpu.VMEM((2, BOTH, 128), bf16),
            pltpu.VMEM((ROWS, BOTH), f32),
            pltpu.VMEM((ROWS, BOTH), bf16),
            pltpu.VMEM((ROWS, BOTH), bf16),
            pltpu.VMEM((2 * NT, BOTH), f32),
            pltpu.VMEM((16, 1, 128), f32),
            pltpu.VMEM((16, 1, 128), f32),
            dma((UNITS,)),
            dma((9,)),
            dma,
            dma((BULK,)),
            dma,
            dma((WIDE, 2)),
            dma,
            dma,
            dma,
            dma,
        ],
        compiler_params=pltpu.CompilerParams(
            collective_id=0, has_side_effects=True, vmem_limit_bytes=63 * 1024 * 1024
        ),
    )(
        eps_corr,
        jnp.swapaxes(pair_rows, 1, 2),
        pair_cols,
        coulomb.reshape(1, OWN),
        wing_row,
        wing_col,
        pair_head,
        head_value,
        head_coulomb,
        inner_bands,
    )


def solution(mesh):
    placed = (
        P(None, "bulk", "wide"),
        P(None, None, ("bulk", "wide")),
        P(None, None, ("wide", "bulk")),
        P(("wide", "bulk")),
        P(None, ("wide", "bulk")),
        P(None, ("bulk", "wide")),
        P(),
        P(),
        P(),
        P(),
    )
    return jax.shard_map(local, mesh=mesh, in_specs=placed, out_specs=P(), check_vma=False)
```

```python
import jax
import jax.numpy as jnp
from jax import lax
from jax.experimental import pallas as pl
from jax.experimental.pallas import tpu as pltpu
from jax.sharding import PartitionSpec as P

NT = 8
NL = 12
NVAL = 12
PAIRS = 96
BOTH = 192
ROWS = 768
COLS = 3072
UNITS = 8
UNIT = 384
OWN = 192
OWN_ROWS = 48
N_Z = 8
WIDE = 16
BULK = 16
BLOCK = 80
CUT = 48
STEPS = (0, 1, -1, 2, -2, 3, -3, 4)
HIGHEST = lax.Precision.HIGHEST
MESH = pl.DeviceIdType.MESH
CONTRACT_LAST = (((1,), (1,)), ((), ()))


def dot(a, b, **kw):
    return jnp.dot(a, b, preferred_element_type=jnp.float32, **kw)


def dot_t(a, b, **kw):
    return lax.dot_general(a, b, CONTRACT_LAST, preferred_element_type=jnp.float32, **kw)


def iota(shape, dim):
    return lax.broadcasted_iota(jnp.int32, shape, dim)


def split(value):
    high = value.astype(jnp.bfloat16)
    return high, (value - high.astype(jnp.float32)).astype(jnp.bfloat16)


def kernel(
    eps_hbm,
    rows_hbm,
    cols_hbm,
    coulomb_hbm,
    wing_row_hbm,
    wing_col_hbm,
    head_hbm,
    head_value_hbm,
    head_coulomb_hbm,
    bands_hbm,
    out_ref,
    eps,
    rows,
    cols,
    coulomb,
    wing_row,
    wing_col,
    head,
    head_value_ref,
    head_coulomb_ref,
    bands_ref,
    parcels,
    own_weighted,
    row_blocks,
    rows_stack,
    rows_turned,
    order,
    fold,
    image,
    image_high,
    image_low,
    base,
    part_a,
    part_b,
    eps_sem,
    in_sem,
    parcel_send,
    parcel_recv,
    row_send,
    row_recv,
    a_send,
    a_recv,
    b_send,
    b_recv,
):
    bulk = lax.axis_index("bulk")
    wide = lax.axis_index("wide")
    core = lax.rem(bulk, 2)
    chip = lax.div(bulk, 2)
    x_lo = lax.div(chip, 4)
    y = lax.rem(chip, 4)
    x_hi = lax.div(wide, N_Z)
    z = lax.rem(wide, N_Z)

    def unit_at(dx, dy):
        return lax.rem(x_lo + dx, 2) * 4 + lax.rem(y + dy, 4)

    def unit_of(i):
        return unit_at(lax.div(i, 4), lax.rem(i, 4))

    def z_at(dz):
        return lax.rem(z + dz + N_Z, N_Z)

    here, across = unit_at(0, 0), unit_at(1, 0)

    def repeat(first, last, step):
        def body(i, carry):
            step(i)
            return carry

        if last - first > 4:
            lax.fori_loop(first, last, body, 0)
        else:
            for i in range(first, last):
                step(i)

    sibling = chip * 2 + 1 - core
    across_x = lax.rem(x_hi + 1, 2) * N_Z + z

    def along_z(dz):
        return x_hi * N_Z + z_at(dz)

    barrier = pltpu.get_barrier_semaphore()

    def greet(to_bulk, to_wide):
        pl.semaphore_signal(barrier, inc=1, device_id={"bulk": to_bulk, "wide": to_wide}, device_id_type=MESH)

    greet(bulk, across_x)
    greet(sibling, wide)
    greet(across * 2 + core, wide)
    for dy in (1, 3, 2):
        greet(unit_at(0, dy) * 2 + core, wide)
    for dz in (1, -1, 2, -2):
        greet(bulk, along_z(dz))

    small = [
        pltpu.make_async_copy(src, dst, in_sem.at[i])
        for i, (src, dst) in enumerate(
            (
                (rows_hbm, rows),
                (cols_hbm, cols),
                (coulomb_hbm, coulomb),
                (head_hbm, head),
                (wing_row_hbm, wing_row),
                (wing_col_hbm, wing_col),
                (head_value_hbm, head_value_ref),
                (head_coulomb_hbm, head_coulomb_ref),
                (bands_hbm, bands_ref),
            )
        )
    ]
    for copy in small[:3]:
        copy.start()

    def slab(i):
        span = pl.ds(pl.multiple_of(unit_of(i) * UNIT, 128), UNIT)
        return pltpu.make_async_copy(eps_hbm.at[:, :, span], eps.at[i], eps_sem.at[i])

    for copy in small[3:]:
        copy.start()

    pl.semaphore_wait(barrier, 10)

    def send(place, send_sem, recv_sem, to_bulk, to_wide):
        pltpu.make_async_remote_copy(
            src_ref=place,
            dst_ref=place,
            send_sem=send_sem,
            recv_sem=recv_sem,
            device_id={"bulk": to_bulk, "wide": to_wide},
            device_id_type=MESH,
        ).start()

    def landed(place, sem):
        pltpu.make_async_copy(place, place, sem).wait()

    def send_parcel(of_bulk, to_bulk):
        send(parcels.at[of_bulk], parcel_send, parcel_recv.at[of_bulk], to_bulk, wide)

    def arrived(unit, of_core):
        at = unit * 2 + of_core
        landed(parcels.at[at], parcel_recv.at[at])

    def hand_on(unit):
        send_parcel(unit * 2 + core, sibling)

    def relay(unit, to_chip):
        send_parcel(unit * 2 + core, to_chip * 2 + core)

    def send_rows(of_wide, to_wide):
        send(row_blocks.at[of_wide], row_send, row_recv.at[of_wide, 0], bulk, to_wide)

    def rows_landed(of_wide):
        landed(row_blocks.at[of_wide], row_recv.at[of_wide, 0])

    small[0].wait()
    rows_f32 = rows[...].astype(jnp.float32)
    rows_own = jnp.concatenate([rows_f32[0], rows_f32[1]], axis=1)
    mine_rows = row_blocks.at[wide]
    rows_low = rows_own.astype(jnp.bfloat16)
    mine_rows[0:48] = rows_low[:, :128]
    packed = jnp.concatenate([rows_own[0:24, 128:], rows_own[24:48, 128:]], axis=1)
    mine_rows[48:80] = jnp.concatenate([packed, jnp.zeros((8, 128), jnp.float32)], axis=0).astype(jnp.bfloat16)
    send_rows(wide, across_x)
    small[1].wait()
    small[2].wait()
    weighted = coulomb[...][None] * cols[...].astype(jnp.float32)
    weighted_pairs = weighted.reshape(BOTH, OWN)
    first = core == 0
    main = jnp.where(first, weighted_pairs[:, 0:128], weighted_pairs[:, 64:192])
    near = jnp.where(first, weighted[0][:, 128:192], weighted[1][:, 0:64])
    far = jnp.where(first, weighted[1][:, 128:192], weighted[0][:, 0:64])
    mine = parcels.at[bulk]
    mine[0:192, :] = main.astype(jnp.bfloat16)
    own_weighted[...] = weighted_pairs.astype(jnp.bfloat16)
    mine[192:288, :] = jnp.concatenate([near, far], axis=1).astype(jnp.bfloat16)


    relay(here, across)

    def send_along(of_wide):
        def step(i):
            send_rows(of_wide, along_z((2, -2, 1, -1)[i]))

        repeat(0, 4, step)

    send_along(wide)
    repeat(1, 4, lambda dy: relay(here, unit_at(0, dy)))
    hand_on(here)
    repeat(0, UNITS, lambda i: slab(i).start())

    low_lanes = iota((PAIRS, 128), 1) < 64

    for copy in small[3:]:
        copy.wait()
    pair_re = head[0:1, :]
    pair_im = head[1:2, :]
    head_row = jnp.concatenate([pair_re, pair_im], axis=1)
    turned_row = jnp.concatenate([-pair_im, pair_re], axis=1)
    coulomb_zero = head_coulomb_ref[0]
    scaled_row = coulomb_zero * head_row
    scaled_turned = coulomb_zero * turned_row
    weighted_low = own_weighted[...]
    weighted_turned = jnp.concatenate([-weighted_low[PAIRS:], weighted_low[:PAIRS]], axis=0)
    wing_cols = wing_row[...]
    gain = dot_t(wing_cols, weighted_low)[0:1] + dot_t(wing_cols, weighted_turned)[1:2]
    tilt = dot(wing_col[...], rows_low)
    leads = jnp.where(jnp.logical_and(bulk == 0, wide == 0), 1.0, 0.0)
    from_head = gain + leads * (head_value_ref[0] * scaled_row + head_value_ref[1] * scaled_turned)
    lane = iota((1, BOTH), 1)
    lane_l = lax.rem(lane, NL)
    lane_band = lax.div(lane, NL)
    weight_row = jnp.zeros((1, BOTH), jnp.float32)
    for l in range(NL):
        weight_row = jnp.where(lane_l == l, jnp.where(bands_ref[l] < NVAL, -0.5, 0.5), weight_row)
    row_at = iota((BOTH, 1), 0)
    same_l = jnp.where(lax.rem(row_at, NL) == lane_l, weight_row, 0.0).astype(jnp.bfloat16)
    in_band = iota((2 * NT, BOTH), 0) == lane_band

    def gathered(row):
        spread = jnp.where(in_band, row, 0.0)
        high = spread.astype(jnp.bfloat16)
        middle, low = split(spread - high.astype(jnp.float32))
        return dot(high, same_l) + dot(middle, same_l) + dot(low, same_l)

    base[...] = (
        gathered(head_row) * from_head + gathered(tilt[0:1]) * scaled_row + gathered(tilt[1:2]) * scaled_turned
    )

    to_lane = iota((1, 128), 1)
    low_part = to_lane < 64
    key = jnp.where(low_part, 0, NT) + lax.rem(to_lane, NT)
    row_band = lax.div(row_at, NL)
    fold[0] = jnp.where(row_band == key, 1.0, 0.0).astype(jnp.bfloat16)
    sign = jnp.where(low_part, 1.0, -1.0)
    fold[1] = jnp.where(row_band == jnp.where(low_part, key + NT, key - NT), sign, 0.0).astype(jnp.bfloat16)
    band_lanes = lax.rem(lax.div(to_lane, NT), NT) == iota((NT, 128), 0)
    lane_half = lax.div(lane, PAIRS)
    place = lane_half * PAIRS + lane_l * NT + lane_band - lane_half * NT
    order[...] = jnp.where(iota((BOTH, BOTH), 0) == place, weight_row, 0.0).astype(jnp.bfloat16)
    image[...] = jnp.zeros((ROWS, BOTH), jnp.float32)

    rows_landed(across_x)
    send_along(across_x)

    @pl.when(core == 0)
    def _():
        arrived(across, core)
        repeat(1, 4, lambda dy: relay(across, unit_at(0, dy)))

    @pl.when(core == 1)
    def _():
        for dy in (1, 3):
            arrived(unit_at(0, dy), core)
            relay(unit_at(0, dy), across)
        arrived(across, core)

    hand_on(across)

    def work(i):
        unit = unit_of(i)
        arrived(unit, 1 - core)
        slab(i).wait()
        head_block = parcels[unit * 2, 0:192, :]
        tail_block = parcels[unit * 2 + 1, 0:192, :]
        half0 = parcels[unit * 2, 192:288, :]
        half1 = parcels[unit * 2 + 1, 192:288, :]
        mid_re = jnp.where(low_lanes, half0, half1)
        mid_im = jnp.where(low_lanes, half1, half0)
        mid_im = jnp.concatenate([mid_im[:, 64:], mid_im[:, :64]], axis=1)
        middle = jnp.concatenate([mid_re, mid_im], axis=0)
        plain = jnp.concatenate([head_block, middle, tail_block], axis=1)
        turned = jnp.concatenate([-plain[PAIRS:], plain[:PAIRS]], axis=0)
        left = jnp.concatenate([eps[i, 0], eps[i, 1]], axis=1)
        right = jnp.concatenate([plain, turned], axis=1)
        for at in range(0, ROWS, 256):
            image[at : at + 256, :] += dot_t(left[at : at + 256], right)

    def relay_rows(at_x):
        for i, dz in enumerate((1, -1)):
            source = at_x * N_Z + z_at(-2 * dz)
            rows_landed(source)
            piece = row_blocks.at[source, pl.ds(0, CUT) if dz == 1 else pl.ds(CUT, BLOCK - CUT)]
            send(piece, row_send, row_recv.at[source, i], bulk, along_z(2 * dz))
            send_rows(source, along_z(dz))

    def second_stage():
        @pl.when(core == 0)
        def _():
            for dy in (1, 2, 3):
                arrived(unit_at(0, dy), core)

        @pl.when(core == 1)
        def _():
            arrived(unit_at(0, 2), core)
            relay(unit_at(0, 2), across)

        relay_rows(x_hi)
        repeat(1, 4, lambda dy: hand_on(unit_at(0, dy)))
        relay_rows(lax.rem(x_hi + 1, 2))

    def third_stage():
        def step(dy):
            arrived(unit_at(1, dy), core)
            hand_on(unit_at(1, dy))

        repeat(1, 4, step)

    def turn_rows(batch):
        for j in range(4 * batch, 4 * batch + 4):
            for half in range(2):
                source = half * N_Z + z_at(STEPS[j])
                at = 96 * j + 48 * half
                packed = row_blocks[source, 48:72, :].astype(jnp.float32)
                rest = jnp.concatenate([packed, pltpu.roll(packed, 64, 1)], axis=0)
                rows_stack[at : at + 48, 0:128] = row_blocks[source, 0:48, :]
                rows_stack[at : at + 48, 128:256] = rest.astype(jnp.bfloat16)
        span = slice(384 * batch, 384 * batch + 384)
        rows_turned[:, span] = dot_t(order[...], rows_stack[span, 0:BOTH]).astype(jnp.bfloat16)

    def units_step(i):
        @pl.when(i == 1)
        def _():
            second_stage()

        @pl.when(i == 3)
        def _():
            third_stage()

        work(i)

    repeat(0, UNITS, units_step)

    for dz in (1, -1):
        for half in range(2):
            rows_landed(half * N_Z + z_at(dz))
    turn_rows(0)

    def split_image(batch):
        for j in range(4 * batch, 4 * batch + 4):
            for half in range(2):
                source = half * N_Z + z_at(STEPS[j])
                at = 96 * j + 48 * half
                block = image[pl.ds(pl.multiple_of(source * OWN_ROWS, 16), OWN_ROWS), :]
                image_high[at : at + 48, :], image_low[at : at + 48, :] = split(block)

    def multiply(batch):
        span = slice(384 * batch, 384 * batch + 384)
        left = rows_turned[:, span]
        return dot(left, image_high[span, :]) + dot(left, image_low[span, :])

    split_image(0)
    split_image(1)
    for half in range(2):
        for dz in (3, -3):
            rows_landed(half * N_Z + z_at(dz))
        source = half * N_Z + z_at(4)
        landed(row_blocks.at[source, pl.ds(0, CUT)], row_recv.at[source, 0])
        landed(row_blocks.at[source, pl.ds(CUT, BLOCK - CUT)], row_recv.at[source, 1])
    turn_rows(1)
    pairs = multiply(0) + multiply(1)
    total = jnp.zeros((NT, 128), jnp.float32)
    for half in range(2):
        kept = jnp.zeros((NT, BOTH), jnp.float32)
        shared = base[NT * half : NT * half + NT, :]
        for l in range(NL):
            at = PAIRS * half + NT * l
            kept = jnp.where(lane_l == l, pairs[at : at + NT, :], kept)
        high, low = split(kept + shared)
        total = total + dot(high, fold[half]) + dot(low, fold[half])
    share = jnp.sum(jnp.where(band_lanes, total, 0.0), axis=0, keepdims=True)

    part_a[bulk] = share

    def others(number, own, step):
        repeat(0, number - 1, lambda k: step(jnp.where(k < own, k, k + 1)))

    others(BULK, bulk, lambda to: send(part_a.at[bulk], a_send, a_recv, to, wide))
    landed(part_a.at[pl.ds(0, BULK - 1)], a_recv)
    part_b[wide] = jnp.sum(part_a[...], axis=0)
    in_order = z * 2 + x_hi
    others(WIDE, in_order, lambda to: send(part_b.at[wide], b_send, b_recv, bulk, lax.rem(to, 2) * N_Z + lax.div(to, 2)))
    landed(parcels.at[pl.ds(0, 15)], parcel_send)
    landed(row_blocks.at[pl.ds(0, 15)], row_send)
    landed(part_a.at[pl.ds(0, BULK - 1)], a_send)
    landed(part_b.at[pl.ds(0, WIDE - 1)], b_recv)
    result = jnp.where(band_lanes, jnp.sum(part_b[...], axis=0), 0.0)
    lanes = iota((NT, 128), 1)
    for part in range(2):
        value = jnp.where(lax.div(lanes, 64) == part, result, 0.0)
        for shift in (8, 16, 32, 64):
            value = value + pltpu.roll(value, shift, 1)
        out_ref[part] = value[:, 0:NT]
    landed(part_b.at[pl.ds(0, WIDE - 1)], b_send)


def local(eps_corr, pair_rows, pair_cols, coulomb, wing_row, wing_col, pair_head, head_value, head_coulomb, inner_bands):
    bf16, f32 = jnp.bfloat16, jnp.float32
    dma = pltpu.SemaphoreType.DMA
    return pl.pallas_call(
        kernel,
        out_shape=jax.ShapeDtypeStruct((2, NT, NT), f32),
        in_specs=[pl.BlockSpec(memory_space=pltpu.HBM)] * 10,
        out_specs=pl.BlockSpec(memory_space=pltpu.VMEM),
        scratch_shapes=[
            pltpu.VMEM((UNITS, 2, ROWS, UNIT), bf16),
            pltpu.VMEM((2, OWN_ROWS, PAIRS), bf16),
            pltpu.VMEM((2, PAIRS, OWN), bf16),
            pltpu.VMEM((1, OWN), f32),
            pltpu.VMEM((2, OWN), bf16),
            pltpu.VMEM((2, OWN_ROWS), bf16),
            pltpu.VMEM((2, PAIRS), f32),
            pltpu.SMEM((2,), f32),
            pltpu.SMEM((1,), f32),
            pltpu.SMEM((NL,), jnp.int32),
            pltpu.VMEM((BULK, 288, 128), bf16),
            pltpu.VMEM((BOTH, OWN), bf16),
            pltpu.VMEM((WIDE, BLOCK, 128), bf16),
            pltpu.VMEM((ROWS, 256), bf16),
            pltpu.VMEM((BOTH, ROWS), bf16),
            pltpu.VMEM((BOTH, BOTH), bf16),
            pltpu.VMEM((2, BOTH, 128), bf16),
            pltpu.VMEM((ROWS, BOTH), f32),
            pltpu.VMEM((ROWS, BOTH), bf16),
            pltpu.VMEM((ROWS, BOTH), bf16),
            pltpu.VMEM((2 * NT, BOTH), f32),
            pltpu.VMEM((16, 1, 128), f32),
            pltpu.VMEM((16, 1, 128), f32),
            dma((UNITS,)),
            dma((9,)),
            dma,
            dma((BULK,)),
            dma,
            dma((WIDE, 2)),
            dma,
            dma,
            dma,
            dma,
        ],
        compiler_params=pltpu.CompilerParams(
            collective_id=0, has_side_effects=True, vmem_limit_bytes=63 * 1024 * 1024
        ),
    )(
        eps_corr,
        jnp.swapaxes(pair_rows, 1, 2),
        pair_cols,
        coulomb.reshape(1, OWN),
        wing_row,
        wing_col,
        pair_head,
        head_value,
        head_coulomb,
        inner_bands,
    )


def solution(mesh):
    placed = (
        P(None, "bulk", "wide"),
        P(None, None, ("bulk", "wide")),
        P(None, None, ("wide", "bulk")),
        P(("wide", "bulk")),
        P(None, ("wide", "bulk")),
        P(None, ("bulk", "wide")),
        P(),
        P(),
        P(),
        P(),
    )
    return jax.shard_map(local, mesh=mesh, in_specs=placed, out_specs=P(), check_vma=False)
```
